256 devices in a mesh: ctx: 64 (over y, x, z_lo, core), head: 4 (over z_hi).
Axes of the slice: x: 4, y: 4, z: 8 (z_hi: 4, z_lo: 2; z = z_hi * 2 + z_lo), core: 2. Of those that a mesh axis runs over, the one named last changes fastest.
Arguments:
- query: bfloat16 [8192, 3072], P('ctx', 'head'), may hold values from -8 to 8
- latent: bfloat16 [8192, 512], P('ctx'), may hold values from -16 to 16
- k_rope: bfloat16 [8192, 64], P('ctx'), may hold values from -8 to 8
- d_out: bfloat16 [8192, 2048], P('ctx', 'head'), may hold values from -6 to 6
- w_kv: bfloat16 [512, 4096], P(None, 'head'), may hold values from -0.25 to 0.25
- block_doc: int32 [64], replicated, may hold values from 0 to 7, never falling along the last dimension, each value on 1 to 36 neighbouring positions
- block_order: int32 [64], replicated, may hold values from 0 to 63, as said below
Outputs:
- d_query: bfloat16 [8192, 3072], P('ctx', 'head')
- d_latent: float32 [8192, 512], P('ctx')
- d_rope: float32 [8192, 64], P('ctx')
- d_w_kv: float32 [512, 4096], P('ctx', 'head')
The draws below stay inside these ranges and needn't reach their ends.
Inputs may be any that keep to these rules, and one draw needn't show every extreme that they name: block_doc never falls along the sequence; every document is a run of 1 to 36 whole blocks and one has exactly 36. `block_order`: each sequence block stands in exactly one slot; the slots of each aligned group of 4 slots hold exactly the sequence blocks of the same indices, in some order.
All inputs are finite; a program needn't handle non-finite values.
Results may differ from the reference program's by a relative error of at most 0.0073.
Values may be sent and summed in bfloat16 or wider, within the bound.
A program may use at most 128 MiB of HBM per device.

```python
import math
import jax
import jax.numpy as jnp
import numpy as np
from jax import lax

LAT = 512
ROPE = 64
NOPE = 128
VDIM = 128
BLK = 128
TOK_DEV = 128
TOKENS = 8192
HEADS = 16
NB = 64
DOCS = 8
DOC_MOST = 36


def draw_query(key, part):
    key = jax.random.fold_in(key, 11)
    drawn_values = jnp.clip(jax.random.normal(key, (TOKENS, HEADS, NOPE + ROPE), jnp.float32), -8.0, 8.0)
    return drawn_values.reshape(TOKENS, HEADS * (NOPE + ROPE)).astype(jnp.bfloat16)


def draw_k_rope(key, part):
    key = jax.random.fold_in(key, 12)
    drawn_values = jnp.clip(jax.random.normal(key, (TOKENS, ROPE), jnp.float32), -8.0, 8.0)
    return drawn_values.astype(jnp.bfloat16)


def draw_block_order(key, part):
    key = jax.random.fold_in(key, 21)
    group_slots = 4 * (TOK_DEV // BLK)
    index_values = jnp.arange(NB, dtype=jnp.int32)
    random_rank = jax.random.randint(key, (NB,), 0, 4096, dtype=jnp.int32)
    score = index_values // group_slots * (4096 * group_slots) + random_rank * group_slots + index_values % group_slots
    return jnp.argsort(score, stable=True).astype(jnp.int32)


def spiked(values, rng, source, target, shards_of, factor):
    owner, partner = [(jnp.arange(values.shape[position]) // (values.shape[position] // shards_of)).reshape([-1 if axis == position else 1 for axis in range(values.ndim)]) for position in (source, target)]
    chosen = jax.random.permutation(rng, shards_of)[partner]
    strong = (owner == chosen) | (owner == (partner + shards_of // 2) % shards_of)
    return jnp.where(strong, factor * values, values)


def levels(stream_key, dims, shards, low, top_value):
    loudness, own = 1.0, jax.random.fold_in(stream_key, 6)
    for axis_at, blocks in shards:
        heights = jnp.exp(jax.random.uniform(jax.random.fold_in(own, axis_at), (blocks,), jnp.float32, low / len(shards), top_value / len(shards)))
        loudness = loudness * jnp.repeat(heights, dims[axis_at] // blocks).reshape([-1 if axis == axis_at else 1 for axis in range(len(dims))])
    return loudness


def split_up(count, total, reach, lean):
    portions = [(1 << 20) // math.isqrt(grade ** lean) + 1 for grade in range(2, count + 1)]
    surplus, counts = total - reach - (count - 1), [1] * (count - 1)
    while surplus > 0:
        candidates = [i for i in range(count - 1) if counts[i] < reach]
        whole, budget = sum([portions[i] for i in candidates]), surplus
        for i in candidates:
            addition = min(reach - counts[i], max(1, budget * portions[i] // whole), surplus)
            counts[i] = counts[i] + addition
            surplus = surplus - addition
    return np.array([reach] + counts)


def ragged_sizes(own_key, count, total, most, slope):
    if count == 2:
        one = jax.random.randint(own_key, (), max(1, total - most), min(most, total - 1) + 1)
        return jnp.stack([one, total - one])
    tallies = jnp.asarray(split_up(count, total, most, slope), jnp.int32)
    twos = (count - 1) // 2
    donor, receiver = tallies[1:1 + 2 * twos:2], tallies[2:2 + 2 * twos:2]
    slack = jnp.minimum(donor - 1, most - receiver)
    shifted = jax.random.randint(jax.random.fold_in(own_key, 1), (twos,), 0, 1 << 20) % (slack + 1)
    tallies = tallies.at[1:1 + 2 * twos:2].set(donor - shifted).at[2:2 + 2 * twos:2].set(receiver + shifted)
    return tallies[jax.random.permutation(jax.random.fold_in(own_key, 2), count)]


def normal_values(key, extent, spread, reach, cuts=(), held_as=jnp.bfloat16):
    factor_of = levels(key, extent, cuts, -0.22, 0.18) if cuts else 1.0
    array = jax.random.normal(key, extent, jnp.float32) * spread * factor_of
    return jnp.minimum(jnp.maximum(array, -reach), reach).astype(held_as)


def heavy_noise(stream_key, shape, spread, most, cuts, heavy, held_as=jnp.bfloat16):
    values = spread * jax.random.normal(stream_key, shape, jnp.float32)
    if cuts:
        values = values * levels(stream_key, shape, cuts, -0.22, 0.18)
    return jnp.clip(spiked(values, jax.random.fold_in(stream_key, 3), *heavy), -most, most).astype(held_as)


def setup_inputs(seed: int = 0) -> dict:
    seeds = jax.random.split(jax.random.key(seed), 8)
    query = draw_query(jax.random.fold_in(seeds[7], 71), 0)
    latent = heavy_noise(seeds[1], (TOKENS, LAT), 1.0, 16.0, ((0, 64),), (0, 1, 64, 4.0))
    k_rope = draw_k_rope(jax.random.fold_in(seeds[7], 71), 0)
    d_out = normal_values(seeds[3], (TOKENS, HEADS * VDIM), 1.0, 6.0, ((0, 64), (1, 4)))
    w_kv = normal_values(seeds[4], (LAT, HEADS * (NOPE + VDIM)), LAT ** -0.5, 0.25, ((1, 4),))
    block_doc = jnp.searchsorted(jnp.cumsum(ragged_sizes(seeds[5], DOCS, NB, DOC_MOST, 2)), jnp.arange(NB), side="right").astype(jnp.int32)
    block_order = draw_block_order(jax.random.fold_in(seeds[7], 71), 0)
    return dict(query=query, latent=latent, k_rope=k_rope, d_out=d_out, w_kv=w_kv, block_doc=block_doc, block_order=block_order)


big_negative = -1e30


def rounded(values):
    return lax.optimization_barrier(values.astype(jnp.bfloat16)).astype(jnp.float32)


def table_lookup(indices, lookup_table):
    entries = lookup_table.shape[0]
    matches = indices[:, None] == jnp.arange(entries, dtype=jnp.int32)[None, :]
    return jnp.sum(jnp.where(matches, lookup_table[None, :], 0), axis=1).astype(jnp.int32)


def inverse_order(block_order):
    entries = block_order.shape[0]
    positions = jnp.arange(entries, dtype=jnp.int32)
    matches = block_order[None, :] == positions[:, None]
    return jnp.sum(jnp.where(matches, positions[None, :], 0), axis=1).astype(jnp.int32)


def reference(query, latent, k_rope, d_out, w_kv, block_doc, block_order):
    highest = lax.Precision.HIGHEST
    head_width = NOPE + ROPE
    pair_width = NOPE + VDIM
    head_count = query.shape[1] // head_width
    score_scale = head_width ** -0.5
    block_count = block_order.shape[0]
    token_count = block_count * BLK
    key_span = 4 * BLK
    step_count = block_count // 4
    shard_blocks = TOK_DEV // BLK
    shard_count = token_count // TOK_DEV
    inverse = inverse_order(block_order)
    seq_latent = jnp.take(latent.reshape(block_count, BLK, LAT), inverse, axis=0).reshape(token_count, LAT)
    seq_rope = jnp.take(k_rope.reshape(block_count, BLK, ROPE), inverse, axis=0).reshape(token_count, ROPE)
    key_value = rounded(jnp.dot(seq_latent, w_kv, preferred_element_type=jnp.float32))
    key_value = key_value.reshape(token_count, head_count, pair_width)
    all_keys = key_value[:, :, :NOPE]
    all_values = key_value[:, :, NOPE:]
    all_rope = seq_rope.astype(jnp.float32)
    key_doc = jnp.repeat(block_doc, BLK)
    offsets = jnp.arange(BLK, dtype=jnp.int32)

    def one_shard(banks, shard_index):
        kv_bank, rope_bank = banks
        row_start = shard_index * TOK_DEV
        parts = lax.dynamic_slice_in_dim(query, row_start, TOK_DEV, 0).astype(jnp.float32)
        parts = parts.reshape(TOK_DEV, head_count, head_width)
        query_nope = parts[:, :, :NOPE]
        query_rope = parts[:, :, NOPE:]
        grad_out = lax.dynamic_slice_in_dim(d_out, row_start, TOK_DEV, 0).astype(jnp.float32)
        grad_out = grad_out.reshape(TOK_DEV, head_count, VDIM)
        shard_order = lax.dynamic_slice_in_dim(block_order, shard_index * shard_blocks, shard_blocks)
        query_pos = (shard_order[:, None] * BLK + offsets[None, :]).reshape(TOK_DEV)
        query_doc = jnp.repeat(table_lookup(shard_order, block_doc), BLK)

        def allowed_at(step_index):
            key_start = step_index * key_span
            docs_here = lax.dynamic_slice_in_dim(key_doc, key_start, key_span)
            pos_here = key_start + jnp.arange(key_span, dtype=jnp.int32)
            return (query_doc[:, None] == docs_here[None, :]) & (pos_here[None, :] <= query_pos[:, None])

        def keys_at(step_index):
            key_start = step_index * key_span
            keys_here = lax.dynamic_slice_in_dim(all_keys, key_start, key_span, 0)
            values_here = lax.dynamic_slice_in_dim(all_values, key_start, key_span, 0)
            rope_here = lax.dynamic_slice_in_dim(all_rope, key_start, key_span, 0)
            return keys_here, values_here, rope_here

        def scores_of(keys_here, rope_here):
            scores = jnp.einsum("qhd,khd->hqk", query_nope, keys_here, precision=highest)
            scores = scores + jnp.einsum("qhd,kd->hqk", query_rope, rope_here, precision=highest)
            return score_scale * scores

        def stats_step(carried, step_index):
            allowed = allowed_at(step_index)

            def live_step(state):
                row_max, mass, weighted = state
                keys_here, values_here, rope_here = keys_at(step_index)
                scores = scores_of(keys_here, rope_here)
                d_probs = jnp.einsum("qhd,khd->hqk", grad_out, values_here, precision=highest)
                new_max = jnp.maximum(row_max, jnp.max(jnp.where(allowed[None], scores, big_negative), axis=2))
                weights = jnp.where(allowed[None], jnp.exp(scores - new_max[:, :, None]), 0.0)
                shrink = jnp.exp(row_max - new_max)
                return new_max, mass * shrink + jnp.sum(weights, axis=2), weighted * shrink + jnp.sum(weights * d_probs, axis=2)

            return lax.cond(jnp.any(allowed), live_step, lambda state: state, carried), None

        start_state = (jnp.full((head_count, TOK_DEV), big_negative, jnp.float32),
                       jnp.zeros((head_count, TOK_DEV), jnp.float32),
                       jnp.zeros((head_count, TOK_DEV), jnp.float32))
        (row_max, mass, weighted), _ = lax.scan(stats_step, start_state, jnp.arange(step_count))
        delta = weighted / mass

        def grad_step(carried, step_index):
            allowed = allowed_at(step_index)

            def live_step(state):
                dq_nope, dq_rope = state
                keys_here, values_here, rope_here = keys_at(step_index)
                scores = scores_of(keys_here, rope_here)
                probs = jnp.where(allowed[None], jnp.exp(scores - row_max[:, :, None]) / mass[:, :, None], 0.0)
                d_probs = jnp.einsum("qhd,khd->hqk", grad_out, values_here, precision=highest)
                mixed = rounded(probs * (d_probs - delta[:, :, None]))
                probs_b = rounded(probs)
                dq_nope = dq_nope + score_scale * jnp.einsum("hqk,khd->qhd", mixed, keys_here, precision=highest)
                dq_rope = dq_rope + score_scale * jnp.einsum("hqk,kd->qhd", mixed, rope_here, precision=highest)
                d_keys = score_scale * jnp.einsum("hqk,qhd->khd", mixed, query_nope, precision=highest)
                d_values = jnp.einsum("hqk,qhd->khd", probs_b, grad_out, precision=highest)
                d_rope_rows = score_scale * jnp.einsum("hqk,qhd->kd", mixed, query_rope, precision=highest)
                d_pairs = rounded(jnp.concatenate([d_keys, d_values], axis=2))
                return (dq_nope, dq_rope), (d_pairs, d_rope_rows)

            def dead_step(state):
                return state, (jnp.zeros((key_span, head_count, pair_width), jnp.float32),
                               jnp.zeros((key_span, ROPE), jnp.float32))

            return lax.cond(jnp.any(allowed), live_step, dead_step, carried)

        start_grads = (jnp.zeros((TOK_DEV, head_count, NOPE), jnp.float32),
                       jnp.zeros((TOK_DEV, head_count, ROPE), jnp.float32))
        (dq_nope, dq_rope), (pair_rows, rope_rows) = lax.scan(grad_step, start_grads, jnp.arange(step_count))
        kv_bank = kv_bank + pair_rows.reshape(token_count, head_count, pair_width)
        rope_bank = rope_bank + rope_rows.reshape(token_count, ROPE)
        dq_shard = jnp.concatenate([dq_nope, dq_rope], axis=2).astype(jnp.bfloat16)
        return (kv_bank, rope_bank), dq_shard.reshape(TOK_DEV, head_count * head_width)

    start_banks = (jnp.zeros((token_count, head_count, pair_width), jnp.float32),
                   jnp.zeros((token_count, ROPE), jnp.float32))
    (kv_bank, rope_bank), dq_all = lax.scan(one_shard, start_banks, jnp.arange(shard_count))
    kv_grad = kv_bank.reshape(token_count, head_count * pair_width)
    d_lat_seq = jnp.dot(kv_grad, w_kv.astype(jnp.float32).T, precision=highest)
    d_w_kv = jnp.dot(seq_latent.astype(jnp.float32).T, kv_grad, precision=highest)
    d_latent = jnp.take(d_lat_seq.reshape(block_count, BLK, LAT), block_order, axis=0).reshape(token_count, LAT)
    d_rope = jnp.take(rope_bank.reshape(block_count, BLK, ROPE), block_order, axis=0).reshape(token_count, ROPE)
    d_query = dq_all.reshape(token_count, head_count * head_width)
    return (d_query, d_latent, d_rope, d_w_kv)
```

```python
import functools
import math

import jax
import jax.numpy as jnp
from jax import lax
from jax.experimental import pallas as pl
from jax.experimental.pallas import tpu as pltpu
from jax.sharding import PartitionSpec as P

LAT = 512
ROPE = 64
NOPE = 128
VDIM = 128
BLK = 128
HEAD = NOPE + ROPE
HALF = BLK // 2
GRP = 4
KEYS = GRP * BLK
ROWS = 2 * BLK + HALF
MOST = 36
SCALE = HEAD**-0.5
LOG2E = math.log2(math.e)
NEG = -1e30
MESH = pl.DeviceIdType.MESH
F32 = jnp.float32
BF16 = jnp.bfloat16


def nt(a, b):
    return lax.dot_general(a, b, (((1,), (1,)), ((), ())), preferred_element_type=F32)


def tn(a, b):
    return lax.dot_general(a, b, (((0,), (0,)), ((), ())), preferred_element_type=F32)


def nn(a, b):
    return jnp.dot(a, b, preferred_element_type=F32)


def pack_halves(rows):
    return jnp.concatenate([rows[:HALF], rows[HALF:]], axis=1)


def unpack_halves(rows):
    return jnp.concatenate([rows[:, :ROPE], rows[:, ROPE:]], axis=0)


def kernel(
    groups,
    zs,
    query,
    latent,
    k_rope,
    d_out,
    w_kv,
    doc,
    order,
    dq_out,
    dlat_out,
    drope_out,
    dw_out,
    kv_stage,
    q_stage,
    kv_buf,
    q_buf,
    lat_buf,
    q_lo,
    q_hi,
    g_out,
    p_buf,
    dp_buf,
    m_ref,
    mass_ref,
    ws_ref,
    fac_ref,
    delta_ref,
    dqn,
    dqr,
    t_send,
    t_recv,
    own_grad,
    kvg,
    kvt,
    dw_send,
    dw_recv,
    dw_sum,
    dw_fin,
    dq_send,
    dq_recv,
    z_send,
    z_recv,
    z_fin,
    s_kv,
    r_kv,
    s_q,
    r_q,
    s_lat,
    r_lat,
    s_blk,
    r_blk,
    s_term,
    r_term,
    s_t,
    r_t,
    s_dw,
    r_dw,
    s_dwf,
    r_dwf,
    s_dq,
    r_dq,
    s_z,
    r_z,
    s_zf,
    r_zf,
):
    ctx = lax.axis_index("ctx")
    hz = lax.axis_index("head")
    g = ctx // GRP
    j = ctx % GRP
    window = min(groups - 1, (MOST + GRP - 2) // GRP)
    w_rows = LAT // groups
    o_rows = w_rows // GRP
    z_rows = BLK // zs
    zp_rows = HALF // zs

    def mate(i):
        return ((g * GRP + (j + i) % GRP), hz)

    def other(i):
        return (((g + i) % groups) * GRP + j, hz)

    def deep(i):
        return (ctx, (hz + i) % zs)

    def remote(src, dst, send, recv, to):
        return pltpu.make_async_remote_copy(
            src_ref=src, dst_ref=dst, send_sem=send, recv_sem=recv, device_id=to, device_id_type=MESH
        )

    barrier = pltpu.get_barrier_semaphore()
    for i in range(1, GRP):
        pl.semaphore_signal(barrier, inc=1, device_id=mate(i), device_id_type=MESH)
    for i in range(1, zs):
        pl.semaphore_signal(barrier, inc=1, device_id=deep(i), device_id_type=MESH)

    def greet(i, carry):
        pl.semaphore_signal(barrier, inc=1, device_id=other(i), device_id_type=MESH)
        return carry

    lax.fori_loop(1, groups, greet, 0)

    kv = nn(latent[...], w_kv[...]).astype(BF16)
    rope_pack = pack_halves(k_rope[...])
    for h in range(GRP):
        kv_stage[h, :BLK] = kv[:, 256 * h : 256 * h + 128]
        kv_stage[h, BLK : 2 * BLK] = kv[:, 256 * h + 128 : 256 * h + 256]
        kv_stage[h, 2 * BLK :] = rope_pack
        q_stage[h, :BLK] = query[:, HEAD * h : HEAD * h + NOPE]
        q_stage[h, BLK : 2 * BLK] = d_out[:, VDIM * h : VDIM * h + VDIM]
        q_stage[h, 2 * BLK :] = pack_halves(query[:, HEAD * h + NOPE : HEAD * h + HEAD])
    lat_buf[j] = latent[...].astype(F32).T.astype(BF16)

    pl.semaphore_wait(barrier, GRP - 1 + zs - 1 + groups - 1)

    def kv_copy(i):
        return remote(kv_stage.at[(j + i) % GRP], kv_buf.at[0, j], s_kv.at[i], r_kv.at[i], mate(i))

    def q_copy(i):
        return remote(q_stage.at[(j + i) % GRP], q_buf.at[j], s_q.at[i], r_q.at[i], mate(i))

    def lat_copy(i):
        return remote(lat_buf.at[j], lat_buf.at[j], s_lat.at[i], r_lat.at[i], mate(i))

    for i in range(1, GRP):
        kv_copy(i).start()
    for i in range(1, GRP):
        q_copy(i).start()
    kv_buf[0, j] = kv_stage[j]
    q_buf[j] = q_stage[j]
    for i in range(1, GRP):
        came = kv_buf.at[0, (j + GRP - i) % GRP]
        remote(came, came, s_kv.at[i], r_kv.at[i], mate(i)).wait_recv()

    def blk_copy(d):
        return remote(kv_buf.at[0], kv_buf.at[d], s_blk.at[d], r_blk.at[d], other(d))

    def send_blk(d, carry):
        @pl.when(g + d < groups)
        def _():
            blk_copy(d).start()

        return carry

    lax.fori_loop(1, window + 1, send_blk, 0)
    for i in range(1, GRP):
        lat_copy(i).start()

    slot_of = lax.broadcasted_iota(jnp.int32, (1, KEYS), 1) // BLK
    in_slot = lax.broadcasted_iota(jnp.int32, (1, KEYS), 1) % BLK
    q_pos = jnp.zeros((1, KEYS), jnp.int32)
    q_doc = jnp.zeros((1, KEYS), jnp.int32)
    for s in range(GRP):
        block = order[GRP * g + s]
        q_pos = jnp.where(slot_of == s, block * BLK + in_slot, q_pos)
        q_doc = jnp.where(slot_of == s, doc[block], q_doc)

    m_ref[...] = jnp.full(m_ref.shape, NEG, F32)
    mass_ref[...] = jnp.zeros(mass_ref.shape, F32)
    ws_ref[...] = jnp.zeros(ws_ref.shape, F32)

    for i in range(1, GRP):
        came = q_buf.at[(j + GRP - i) % GRP]
        remote(came, came, s_q.at[i], r_q.at[i], mate(i)).wait_recv()
    blank = jnp.zeros((HALF, ROPE), BF16)
    for s in range(GRP):
        at = s * BLK
        pair = q_buf[s, 2 * BLK :]
        first, second = pair[:, :ROPE], pair[:, ROPE:]
        q_lo[at : at + BLK, :NOPE] = q_buf[s, :BLK]
        q_hi[at : at + BLK, :NOPE] = q_buf[s, :BLK]
        g_out[at : at + BLK] = q_buf[s, BLK : 2 * BLK]
        q_lo[at : at + HALF, NOPE:] = jnp.concatenate([first, blank], axis=1)
        q_lo[at + HALF : at + BLK, NOPE:] = jnp.concatenate([second, blank], axis=1)
        q_hi[at : at + HALF, NOPE:] = jnp.concatenate([blank, first], axis=1)
        q_hi[at + HALF : at + BLK, NOPE:] = jnp.concatenate([blank, second], axis=1)

    def gather_rows(d, low):
        return jnp.concatenate([kv_buf[d, s, low : low + HALF] for s in range(GRP)], axis=0)

    def keys_of(d, half):
        return jnp.concatenate([gather_rows(d, half * HALF), gather_rows(d, 2 * BLK)], axis=1)

    def scores_tile(d, local):
        top = jnp.full((8, KEYS), NEG, F32)
        for half in range(2):
            scores = nt(keys_of(d, half), (q_lo, q_hi)[half][...])
            for s in range(GRP):
                block = order[GRP * (g - d) + s]
                same = q_doc == doc[block]
                part = scores[s * HALF : s * HALF + HALF] * (SCALE * LOG2E)
                if local:
                    pos = lax.broadcasted_iota(jnp.int32, (HALF, 1), 0) + (block * BLK + half * HALF)
                    part = jnp.where(same & (pos <= q_pos), part, NEG)
                else:
                    part = part + jnp.where(same, 0.0, NEG)
                p_buf[d, half, s] = part
                top = jnp.maximum(top, jnp.max(part.reshape(HALF // 8, 8, KEYS), axis=0))
        peak = jnp.max(top, axis=0, keepdims=True)
        mass = jnp.zeros((8, KEYS), F32)
        weighted = jnp.zeros((8, KEYS), F32)
        for half in range(2):
            dp = nt(gather_rows(d, BLK + half * HALF), g_out[...])
            for s in range(GRP):
                here = dp[s * HALF : s * HALF + HALF]
                p = jnp.exp2(p_buf[d, half, s] - peak)
                p_buf[d, half, s] = p
                dp_buf[d, half, s] = here
                mass = mass + jnp.sum(p.reshape(HALF // 8, 8, KEYS), axis=0)
                weighted = weighted + jnp.sum((p * here).reshape(HALF // 8, 8, KEYS), axis=0)
        m_ref[d] = peak
        mass_ref[d] = jnp.sum(mass, axis=0, keepdims=True)
        ws_ref[d] = jnp.sum(weighted, axis=0, keepdims=True)

    scores_tile(0, True)

    def far_scores(d, carry):
        @pl.when(g >= d)
        def _():
            came = kv_buf.at[d]
            remote(came, came, s_blk.at[d], r_blk.at[d], other(d)).wait_recv()
            scores_tile(d, False)

        return carry

    lax.fori_loop(1, window + 1, far_scores, 0)

    peak = jnp.max(m_ref[...], axis=0)
    factors = jnp.exp2(m_ref[...] - peak[None])
    mass = jnp.sum(mass_ref[...] * factors, axis=0)
    weighted = jnp.sum(ws_ref[...] * factors, axis=0)
    fac_ref[...] = factors / mass[None]
    delta_ref[...] = weighted / mass
    dqn[...] = jnp.zeros(dqn.shape, F32)
    dqr[...] = jnp.zeros(dqr.shape, F32)

    def grads_tile(d, put):
        factor = fac_ref[d]
        delta = delta_ref[...]
        rope_sum = None
        for half in range(2):
            mixed, probs = [], []
            for s in range(GRP):
                p = p_buf[d, half, s] * factor
                mixed.append((p * (dp_buf[d, half, s] - delta)).astype(BF16))
                probs.append(p.astype(BF16))
            mixed = jnp.concatenate(mixed, axis=0)
            probs = jnp.concatenate(probs, axis=0)
            d_keys = nn(mixed, (q_lo, q_hi)[half][...]) * SCALE
            d_values = nn(probs, g_out[...])
            rope_sum = d_keys[:, NOPE:] if half == 0 else rope_sum + d_keys[:, NOPE:]
            for s in range(GRP):
                put(s, half * HALF, d_keys[s * HALF : s * HALF + HALF, :NOPE])
                put(s, BLK + half * HALF, d_values[s * HALF : s * HALF + HALF])
            dq = tn(keys_of(d, half), mixed)
            dqn[...] += dq[:NOPE]
            dqr[...] += dq[NOPE + half * ROPE : NOPE + half * ROPE + ROPE]
        for s in range(GRP):
            put(s, 2 * BLK, rope_sum[s * HALF : s * HALF + HALF])

    def term_copy(d):
        return remote(t_send.at[d], t_recv.at[d], s_term.at[d], r_term.at[d], other(groups - d))

    def far_grads(step, carry):
        d = window - step

        @pl.when(g >= d)
        def _():
            def put(s, low, rows):
                t_send[d, s, low : low + HALF] = rows.astype(BF16)

            grads_tile(d, put)
            term_copy(d).start()

        return carry

    lax.fori_loop(0, window, far_grads, 0)

    def put_own(s, low, rows):
        own_grad[s, low : low + HALF] = rows

    grads_tile(0, put_own)

    dq_nope = (dqn[...] * SCALE).T.astype(BF16)
    dq_rope = (dqr[...] * SCALE).T.astype(BF16)
    for s in range(GRP):
        dq_send[s, :BLK] = dq_nope[s * BLK : s * BLK + BLK]
        dq_send[s, BLK:] = pack_halves(dq_rope[s * BLK : s * BLK + BLK])
    dq_recv[j] = dq_send[j]

    def dq_copy(i):
        return remote(dq_send.at[(j + i) % GRP], dq_recv.at[j], s_dq.at[i], r_dq.at[i], mate(i))

    for i in range(1, GRP):
        dq_copy(i).start()

    def take_terms(d, carry):
        @pl.when(g + d < groups)
        def _():
            came = t_recv.at[d]
            remote(came, came, s_term.at[d], r_term.at[d], other(d)).wait_recv()
            own_grad[...] += t_recv[d].astype(F32)

        return carry

    lax.fori_loop(1, window + 1, take_terms, 0)
    kvg[...] = own_grad[...].astype(BF16)
    kvt[j] = kvg[j]

    def t_copy(i):
        return remote(kvg.at[(j + i) % GRP], kvt.at[j], s_t.at[i], r_t.at[i], mate(i))

    for i in range(1, GRP):
        t_copy(i).start()

    for i in range(1, GRP):
        came = lat_buf.at[(j + GRP - i) % GRP]
        remote(came, came, s_lat.at[i], r_lat.at[i], mate(i)).wait_recv()
    grad_w = jnp.zeros((LAT, NOPE + VDIM), F32)
    for s in range(GRP):
        pair = jnp.concatenate([kvg[s, :BLK], kvg[s, BLK : 2 * BLK]], axis=1)
        grad_w = grad_w + nn(lat_buf[s], pair)
    grad_w = grad_w.astype(BF16)
    for i in range(groups):
        dw_send[i] = grad_w[i * w_rows : (i + 1) * w_rows]

    def dw_copy(i):
        return remote(dw_send.at[(g + i) % groups], dw_recv.at[i], s_dw.at[i], r_dw.at[i], other(i))

    def send_dw(i, carry):
        dw_copy(i).start()
        return carry

    lax.fori_loop(1, groups, send_dw, 0)

    for i in range(1, GRP):
        came = kvt.at[(j + GRP - i) % GRP]
        remote(came, came, s_t.at[i], r_t.at[i], mate(i)).wait_recv()
    pairs = jnp.concatenate(
        [kvt[h, low : low + BLK] for h in range(GRP) for low in (0, BLK)], axis=1
    )
    d_lat = nt(pairs, w_kv[...])
    d_rope = kvt[0, 2 * BLK :].astype(F32)
    for h in range(1, GRP):
        d_rope = d_rope + kvt[h, 2 * BLK :].astype(F32)
    for t in range(zs):
        z_send[t, :, :LAT] = d_lat[t * z_rows : (t + 1) * z_rows].astype(BF16)
        z_send[t, :zp_rows, LAT:] = d_rope[t * zp_rows : (t + 1) * zp_rows].astype(BF16)
        z_send[t, zp_rows:, LAT:] = jnp.zeros((z_rows - zp_rows, 2 * ROPE), BF16)

    def z_copy(i):
        return remote(z_send.at[(hz + i) % zs], z_recv.at[i], s_z.at[i], r_z.at[i], deep(i))

    for i in range(1, zs):
        z_copy(i).start()

    for i in range(1, GRP):
        came = dq_recv.at[(j + GRP - i) % GRP]
        remote(came, came, s_dq.at[i], r_dq.at[i], mate(i)).wait_recv()
    columns = []
    for h in range(GRP):
        columns += [dq_recv[h, :BLK], unpack_halves(dq_recv[h, BLK:])]
    dq_out[...] = jnp.concatenate(columns, axis=1)

    z_sum = z_send[hz].astype(F32)
    for i in range(1, zs):
        remote(z_recv.at[i], z_recv.at[i], s_z.at[i], r_z.at[i], deep(i)).wait_recv()
        z_sum = z_sum + z_recv[i].astype(F32)
    z_fin[hz] = z_sum.astype(BF16)

    def zf_copy(i):
        return remote(z_fin.at[hz], z_fin.at[hz], s_zf.at[i], r_zf.at[i], deep(i))

    for i in range(1, zs):
        zf_copy(i).start()

    dw_sum[...] = dw_send[g].astype(F32)

    def take_dw(i, carry):
        remote(dw_recv.at[i], dw_recv.at[i], s_dw.at[i], r_dw.at[i], other(i)).wait_recv()
        dw_sum[...] += dw_recv[i].astype(F32)
        return carry

    lax.fori_loop(1, groups, take_dw, 0)

    def dwf_copy(i):
        rows = pl.ds(pl.multiple_of((j + i) % GRP * o_rows, o_rows), o_rows)
        return remote(dw_sum.at[rows], dw_fin.at[j], s_dwf.at[i], r_dwf.at[i], mate(i))

    for i in range(1, GRP):
        dwf_copy(i).start()
    dw_fin[j] = dw_sum[pl.ds(pl.multiple_of(j * o_rows, o_rows), o_rows)]

    for i in range(1, zs):
        came = z_fin.at[(hz + zs - i) % zs]
        remote(came, came, s_zf.at[i], r_zf.at[i], deep(i)).wait_recv()
    packed = []
    for t in range(zs):
        dlat_out[t * z_rows : (t + 1) * z_rows] = z_fin[t, :, :LAT].astype(F32)
        packed.append(z_fin[t, :zp_rows, LAT:].astype(F32))
    drope_out[...] = unpack_halves(jnp.concatenate(packed, axis=0))

    for i in range(1, GRP):
        came = dw_fin.at[(j + GRP - i) % GRP]
        remote(came, came, s_dwf.at[i], r_dwf.at[i], mate(i)).wait_recv()
    dw_out[...] = jnp.concatenate([dw_fin[h] for h in range(GRP)], axis=1)

    for i in range(1, GRP):
        kv_copy(i).wait_send()
        q_copy(i).wait_send()
        lat_copy(i).wait_send()
        dq_copy(i).wait_send()
        t_copy(i).wait_send()
        dwf_copy(i).wait_send()
    for i in range(1, zs):
        z_copy(i).wait_send()
        zf_copy(i).wait_send()

    def end_far(d, carry):
        @pl.when(g + d < groups)
        def _():
            blk_copy(d).wait_send()

        @pl.when(g >= d)
        def _():
            term_copy(d).wait_send()

        return carry

    lax.fori_loop(1, window + 1, end_far, 0)

    def end_dw(i, carry):
        dw_copy(i).wait_send()
        return carry

    lax.fori_loop(1, groups, end_dw, 0)


def solution(mesh):
    groups = mesh.shape["ctx"] // GRP
    zs = mesh.shape["head"]
    span = min(groups - 1, (MOST + GRP - 2) // GRP) + 1
    w_rows = LAT // groups
    z_rows = BLK // zs
    vmem = pltpu.VMEM
    dma = pltpu.SemaphoreType.DMA
    scratch = [
        vmem((GRP, ROWS, 128), BF16),
        vmem((GRP, ROWS, 128), BF16),
        vmem((span, GRP, ROWS, 128), BF16),
        vmem((GRP, ROWS, 128), BF16),
        vmem((GRP, LAT, BLK), BF16),
        vmem((KEYS, 256), BF16),
        vmem((KEYS, 256), BF16),
        vmem((KEYS, VDIM), BF16),
        vmem((span, 2, GRP, HALF, KEYS), F32),
        vmem((span, 2, GRP, HALF, KEYS), F32),
        vmem((span, 1, KEYS), F32),
        vmem((span, 1, KEYS), F32),
        vmem((span, 1, KEYS), F32),
        vmem((span, 1, KEYS), F32),
        vmem((1, KEYS), F32),
        vmem((NOPE, KEYS), F32),
        vmem((ROPE, KEYS), F32),
        vmem((span, GRP, ROWS, 128), BF16),
        vmem((span, GRP, ROWS, 128), BF16),
        vmem((GRP, ROWS, 128), F32),
        vmem((GRP, ROWS, 128), BF16),
        vmem((GRP, ROWS, 128), BF16),
        vmem((groups, w_rows, 256), BF16),
        vmem((groups, w_rows, 256), BF16),
        vmem((w_rows, 256), F32),
        vmem((GRP, w_rows // GRP, 256), F32),
        vmem((GRP, BLK + HALF, 128), BF16),
        vmem((GRP, BLK + HALF, 128), BF16),
        vmem((zs, z_rows, LAT + 128), BF16),
        vmem((zs, z_rows, LAT + 128), BF16),
        vmem((zs, z_rows, LAT + 128), BF16),
    ]
    for count in (GRP, GRP, GRP, span, span, GRP, groups, GRP, GRP, zs, zs):
        scratch += [dma((count,)), dma((count,))]

    def local(query, latent, k_rope, d_out, w_kv, block_doc, block_order):
        whole = pl.BlockSpec(memory_space=pltpu.VMEM)
        scalars = pl.BlockSpec(memory_space=pltpu.SMEM)
        return pl.pallas_call(
            functools.partial(kernel, groups, zs),
            out_shape=(
                jax.ShapeDtypeStruct(query.shape, BF16),
                jax.ShapeDtypeStruct((BLK, LAT), F32),
                jax.ShapeDtypeStruct((BLK, ROPE), F32),
                jax.ShapeDtypeStruct((w_rows // GRP, GRP * 256), F32),
            ),
            in_specs=[whole] * 5 + [scalars] * 2,
            out_specs=(whole,) * 4,
            scratch_shapes=scratch,
            compiler_params=pltpu.CompilerParams(
                collective_id=0, has_side_effects=True, vmem_limit_bytes=56 * 1024 * 1024
            ),
        )(query, latent, k_rope, d_out, w_kv, block_doc, block_order)

    return jax.shard_map(
        local,
        mesh=mesh,
        in_specs=(
            P("ctx", "head"),
            P("ctx", None),
            P("ctx", None),
            P("ctx", "head"),
            P(None, "head"),
            P(),
            P(),
        ),
        out_specs=(P("ctx", "head"), P("ctx", None), P("ctx", None), P("ctx", "head")),
        check_vma=False,
    )
```

```python
import functools
import math

import jax
import jax.numpy as jnp
from jax import lax
from jax.experimental import pallas as pl
from jax.experimental.pallas import tpu as pltpu
from jax.sharding import PartitionSpec as P

LAT = 512
ROPE = 64
NOPE = 128
VDIM = 128
BLK = 128
HEAD = NOPE + ROPE
HALF = BLK // 2
GRP = 4
KEYS = GRP * BLK
ROWS = 2 * BLK + HALF
COLS = LAT // BLK
PIECE = LAT + HALF
MOST = 36
SCALE = HEAD**-0.5
LOG2E = math.log2(math.e)
NEG = -1e30
MESH = pl.DeviceIdType.MESH
F32 = jnp.float32
BF16 = jnp.bfloat16


def nt(a, b):
    return lax.dot_general(a, b, (((1,), (1,)), ((), ())), preferred_element_type=F32)


def tn(a, b):
    return lax.dot_general(a, b, (((0,), (0,)), ((), ())), preferred_element_type=F32)


def nn(a, b):
    return jnp.dot(a, b, preferred_element_type=F32)


def pack_halves(rows):
    return jnp.concatenate([rows[:HALF], rows[HALF:]], axis=1)


def unpack_halves(rows):
    return jnp.concatenate([rows[:, :ROPE], rows[:, ROPE:]], axis=0)


def kernel(
    groups,
    zs,
    query,
    latent,
    k_rope,
    d_out,
    w_kv,
    doc,
    order,
    dq_out,
    dlat_out,
    drope_out,
    dw_out,
    q_stage,
    q_buf,
    lat_buf,
    k_buf,
    w_head,
    q_lo,
    q_hi,
    g_out,
    p_buf,
    dp_buf,
    m_ref,
    mass_ref,
    ws_ref,
    fac_ref,
    delta_ref,
    dqn,
    dqr,
    dw_acc,
    terms,
    core_recv,
    near_send,
    near_recv,
    far_send,
    far_recv,
    total,
    dw_send,
    dw_recv,
    dw_sum,
    dw_fin,
    dq_send,
    dq_recv,
    z_send,
    z_recv,
    z_fin,
    s_q,
    r_q,
    s_far,
    r_far,
    s_own,
    r_own,
    s_near,
    r_near,
    s_pass,
    r_pass,
    s_tc,
    r_tc,
    s_tx,
    r_tx,
    s_tn,
    r_tn,
    s_tf,
    r_tf,
    s_dw,
    r_dw,
    s_dwf,
    r_dwf,
    s_dq,
    r_dq,
    s_z,
    r_z,
    s_zf,
    r_zf,
):
    ctx = lax.axis_index("ctx")
    hz = lax.axis_index("head")
    g = ctx // GRP
    j = ctx % GRP
    z_lo = j // 2
    core = j % 2
    j_core = 2 * z_lo + 1 - core
    j_near = 2 * (1 - z_lo) + core
    j_next = 2 * (1 - z_lo) + 1 - core
    window = min(groups - 1, (MOST + GRP - 2) // GRP)
    w_rows = LAT // groups
    o_rows = w_rows // GRP
    z_rows = BLK // zs
    zp_rows = HALF // zs

    def mate(i):
        return ((g * GRP + (j + i) % GRP), hz)

    def other(i):
        return (((g + i) % groups) * GRP + j, hz)

    def deep(i):
        return (ctx, (hz + i) % zs)

    beside = (g * GRP + j_core, hz)
    ahead = (g * GRP + j_near, (hz + z_lo + core * (zs - 1)) % zs)
    behind = (g * GRP + j_near, (hz + z_lo + (1 - core) * (zs - 1)) % zs)

    def remote(src, dst, send, recv, to):
        return pltpu.make_async_remote_copy(
            src_ref=src, dst_ref=dst, send_sem=send, recv_sem=recv, device_id=to, device_id_type=MESH
        )

    def arrived(ref, sem, to):
        remote(ref, ref, sem, sem, to).wait_recv()

    barrier = pltpu.get_barrier_semaphore()
    for i in range(1, GRP):
        pl.semaphore_signal(barrier, inc=1, device_id=mate(i), device_id_type=MESH)
    for i in range(1, zs):
        pl.semaphore_signal(barrier, inc=1, device_id=deep(i), device_id_type=MESH)
    pl.semaphore_signal(barrier, inc=1, device_id=ahead, device_id_type=MESH)
    pl.semaphore_signal(barrier, inc=1, device_id=behind, device_id_type=MESH)

    def greet(i, carry):
        pl.semaphore_signal(barrier, inc=1, device_id=other(i), device_id_type=MESH)
        return carry

    lax.fori_loop(1, groups, greet, 0)

    for c in range(COLS):
        lat_buf[0, j, c * BLK : (c + 1) * BLK] = latent[:, c * BLK : (c + 1) * BLK]
    lat_buf[0, j, LAT:] = pack_halves(k_rope[...].astype(F32).T.astype(BF16))
    for h in range(GRP):
        q_stage[h, :BLK] = query[:, HEAD * h : HEAD * h + NOPE]
        q_stage[h, BLK : 2 * BLK] = d_out[:, VDIM * h : VDIM * h + VDIM]
        q_stage[h, 2 * BLK :] = pack_halves(query[:, HEAD * h + NOPE : HEAD * h + HEAD])

    pl.semaphore_wait(barrier, GRP - 1 + zs - 1 + 2 + groups - 1)

    def far_copy(d):
        return remote(lat_buf.at[0, j], lat_buf.at[d, j], s_far.at[d], r_far.at[d], other(d))

    def own_copy(d):
        return remote(lat_buf.at[d, j], lat_buf.at[d, j], s_own.at[d], r_own.at[d], beside)

    def near_copy(d):
        return remote(lat_buf.at[d, j], lat_buf.at[d, j], s_near.at[d], r_near.at[d], ahead)

    def pass_copy(d):
        return remote(lat_buf.at[d, j_near], lat_buf.at[d, j_near], s_pass.at[d], r_pass.at[d], beside)

    def q_copy(i):
        return remote(q_stage.at[(j + i) % GRP], q_buf.at[j], s_q.at[i], r_q.at[i], mate(i))

    def send_far(d, carry):
        @pl.when(g + d < groups)
        def _():
            far_copy(d).start()

        return carry

    near_copy(0).start()
    own_copy(0).start()
    lax.fori_loop(1, window + 1, send_far, 0)
    for i in range(1, GRP):
        q_copy(i).start()
    q_buf[j] = q_stage[j]
    w_head[...] = w_kv[:, pl.ds(pl.multiple_of(j * 256, 256), 256)]

    slot_of = lax.broadcasted_iota(jnp.int32, (1, KEYS), 1) // BLK
    in_slot = lax.broadcasted_iota(jnp.int32, (1, KEYS), 1) % BLK
    q_pos = jnp.zeros((1, KEYS), jnp.int32)
    q_doc = jnp.zeros((1, KEYS), jnp.int32)
    for s in range(GRP):
        block = order[GRP * g + s]
        q_pos = jnp.where(slot_of == s, block * BLK + in_slot, q_pos)
        q_doc = jnp.where(slot_of == s, doc[block], q_doc)

    m_ref[...] = jnp.full(m_ref.shape, NEG, F32)
    mass_ref[...] = jnp.zeros(mass_ref.shape, F32)
    ws_ref[...] = jnp.zeros(ws_ref.shape, F32)

    def latents_of(d):
        return jnp.concatenate(
            [
                jnp.concatenate([lat_buf[d, s, c * BLK : (c + 1) * BLK] for c in range(COLS)], axis=1)
                for s in range(GRP)
            ],
            axis=0,
        )

    def half_rows(rows, half):
        return jnp.concatenate(
            [rows[s * BLK + half * HALF : s * BLK + half * HALF + HALF] for s in range(GRP)], axis=0
        )

    def scores_tile(d, local):
        kv = nn(latents_of(d), w_head[...]).astype(BF16)
        rope = jnp.concatenate([lat_buf[d, s, LAT:] for s in range(GRP)], axis=0)
        top = jnp.full((8, KEYS), NEG, F32)
        for half in range(2):
            k_buf[d, half] = jnp.concatenate([half_rows(kv[:, :NOPE], half), rope], axis=1)
            scores = nt(k_buf[d, half], (q_lo, q_hi)[half][...])
            for s in range(GRP):
                block = order[GRP * (g - d) + s]
                same = q_doc == doc[block]
                part = scores[s * HALF : s * HALF + HALF] * (SCALE * LOG2E)
                if local:
                    pos = lax.broadcasted_iota(jnp.int32, (HALF, 1), 0) + (block * BLK + half * HALF)
                    part = jnp.where(same & (pos <= q_pos), part, NEG)
                else:
                    part = part + jnp.where(same, 0.0, NEG)
                p_buf[d, half, s] = part
                top = jnp.maximum(top, jnp.max(part.reshape(HALF // 8, 8, KEYS), axis=0))
        peak = jnp.max(top, axis=0, keepdims=True)
        mass = jnp.zeros((8, KEYS), F32)
        weighted = jnp.zeros((8, KEYS), F32)
        for half in range(2):
            dp = nt(half_rows(kv[:, NOPE:], half), g_out[...])
            for s in range(GRP):
                here = dp[s * HALF : s * HALF + HALF]
                p = jnp.exp2(p_buf[d, half, s] - peak)
                p_buf[d, half, s] = p
                dp_buf[d, half, s] = here
                mass = mass + jnp.sum(p.reshape(HALF // 8, 8, KEYS), axis=0)
                weighted = weighted + jnp.sum((p * here).reshape(HALF // 8, 8, KEYS), axis=0)
        m_ref[d] = peak
        mass_ref[d] = jnp.sum(mass, axis=0, keepdims=True)
        ws_ref[d] = jnp.sum(weighted, axis=0, keepdims=True)

    def spread(d):
        @pl.when((d <= window) & (g >= d))
        def _():
            arrived(lat_buf.at[d, j], r_far.at[d], beside)
            near_copy(d).start()
            own_copy(d).start()

    def hand_on(d):
        @pl.when((d <= window) & (g >= d))
        def _():
            arrived(lat_buf.at[d, j_near], r_near.at[d], beside)
            pass_copy(d).start()

    def whole(d):
        arrived(lat_buf.at[d, j_core], r_own.at[d], beside)
        arrived(lat_buf.at[d, j_next], r_pass.at[d], beside)

    hand_on(0)
    for i in range(1, GRP):
        arrived(q_buf.at[(j + GRP - i) % GRP], r_q.at[i], mate(i))
    blank = jnp.zeros((HALF, ROPE), BF16)
    for s in range(GRP):
        at = s * BLK
        pair = q_buf[s, 2 * BLK :]
        first, second = pair[:, :ROPE], pair[:, ROPE:]
        q_lo[at : at + BLK, :NOPE] = q_buf[s, :BLK]
        q_hi[at : at + BLK, :NOPE] = q_buf[s, :BLK]
        g_out[at : at + BLK] = q_buf[s, BLK : 2 * BLK]
        q_lo[at : at + HALF, NOPE:] = jnp.concatenate([first, blank], axis=1)
        q_lo[at + HALF : at + BLK, NOPE:] = jnp.concatenate([second, blank], axis=1)
        q_hi[at : at + HALF, NOPE:] = jnp.concatenate([blank, first], axis=1)
        q_hi[at + HALF : at + BLK, NOPE:] = jnp.concatenate([blank, second], axis=1)
    spread(1)
    whole(0)
    scores_tile(0, True)

    def far_scores(i, carry):
        spread(i)
        hand_on(i - 1)

        @pl.when(g >= i - 2)
        def _():
            whole(i - 2)
            scores_tile(i - 2, False)

        return carry

    spread(2)
    hand_on(1)
    lax.fori_loop(3, window + 3, far_scores, 0)

    peak = jnp.max(m_ref[...], axis=0)
    factors = jnp.exp2(m_ref[...] - peak[None])
    mass = jnp.sum(mass_ref[...] * factors, axis=0)
    weighted = jnp.sum(ws_ref[...] * factors, axis=0)
    fac_ref[...] = factors / mass[None]
    delta_ref[...] = weighted / mass
    dqn[...] = jnp.zeros(dqn.shape, F32)
    dqr[...] = jnp.zeros(dqr.shape, F32)
    dw_acc[...] = jnp.zeros(dw_acc.shape, F32)

    def grads_tile(d):
        factor = fac_ref[d]
        delta = delta_ref[...]
        rope_sum = None
        pairs = []
        for half in range(2):
            mixed, probs = [], []
            for s in range(GRP):
                p = p_buf[d, half, s] * factor
                mixed.append((p * (dp_buf[d, half, s] - delta)).astype(BF16))
                probs.append(p.astype(BF16))
            mixed = jnp.concatenate(mixed, axis=0)
            probs = jnp.concatenate(probs, axis=0)
            d_keys = nn(mixed, (q_lo, q_hi)[half][...]) * SCALE
            d_values = nn(probs, g_out[...])
            rope_sum = d_keys[:, NOPE:] if half == 0 else rope_sum + d_keys[:, NOPE:]
            pairs.append(jnp.concatenate([d_keys[:, :NOPE], d_values], axis=1).astype(BF16))
            dq = tn(k_buf[d, half], mixed)
            dqn[...] += dq[:NOPE]
            dqr[...] += dq[NOPE + half * ROPE : NOPE + half * ROPE + ROPE]
        pairs = jnp.concatenate(
            [pairs[half][s * HALF : s * HALF + HALF] for s in range(GRP) for half in range(2)], axis=0
        )
        d_lat = nt(pairs, w_head[...])
        for s in range(GRP):
            for c in range(COLS):
                part = d_lat[s * BLK : (s + 1) * BLK, c * BLK : (c + 1) * BLK]
                terms[d, s, c * BLK : (c + 1) * BLK] = part.astype(BF16)
            terms[d, s, LAT:] = rope_sum[s * HALF : s * HALF + HALF].astype(BF16)
        dw_acc[...] += tn(pairs, latents_of(d))

    def tc_copy(d):
        return remote(terms.at[d, j_core], core_recv.at[d, 0], s_tc.at[d], r_tc.at[d], beside)

    def tx_copy(d):
        return remote(terms.at[d, j_next], core_recv.at[d, 1], s_tx.at[d], r_tx.at[d], beside)

    def tn_copy(d):
        return remote(near_send.at[d], near_recv.at[d], s_tn.at[d], r_tn.at[d], behind)

    def tf_copy(d):
        return remote(far_send.at[d], far_recv.at[d], s_tf.at[d], r_tf.at[d], other(groups - d))

    def chip_sum(d):
        @pl.when((d <= window) & (g >= d))
        def _():
            arrived(core_recv.at[d, 1], r_tx.at[d], beside)
            near_send[d] = (terms[d, j_near].astype(F32) + core_recv[d, 1].astype(F32)).astype(BF16)
            tn_copy(d).start()

    def slot_sum(d):
        arrived(core_recv.at[d, 0], r_tc.at[d], beside)
        arrived(near_recv.at[d], r_tn.at[d], beside)
        return terms[d, j].astype(F32) + core_recv[d, 0].astype(F32) + near_recv[d].astype(F32)

    def send_terms(d):
        @pl.when((d <= window) & (g >= d))
        def _():
            far_send[d] = slot_sum(d).astype(BF16)
            tf_copy(d).start()

    def far_grads(step, carry):
        d = window - step

        @pl.when(g >= d)
        def _():
            grads_tile(d)
            tx_copy(d).start()
            tc_copy(d).start()

        chip_sum(d + 1)
        send_terms(d + 2)
        return carry

    lax.fori_loop(0, window + 1, far_grads, 0)
    chip_sum(0)
    send_terms(1)

    dq_nope = (dqn[...] * SCALE).T.astype(BF16)
    dq_rope = (dqr[...] * SCALE).T.astype(BF16)
    for s in range(GRP):
        dq_send[s, :BLK] = dq_nope[s * BLK : s * BLK + BLK]
        dq_send[s, BLK:] = pack_halves(dq_rope[s * BLK : s * BLK + BLK])
    dq_recv[j] = dq_send[j]

    def dq_copy(i):
        return remote(dq_send.at[(j + i) % GRP], dq_recv.at[j], s_dq.at[i], r_dq.at[i], mate(i))

    for i in range(1, GRP):
        dq_copy(i).start()

    grad_w = dw_acc[...].T.astype(BF16)
    for i in range(groups):
        dw_send[i] = grad_w[i * w_rows : (i + 1) * w_rows]

    def dw_copy(i):
        return remote(dw_send.at[(g + i) % groups], dw_recv.at[i], s_dw.at[i], r_dw.at[i], other(i))

    def send_dw(i, carry):
        dw_copy(i).start()
        return carry

    lax.fori_loop(1, groups, send_dw, 0)

    total[...] = slot_sum(0)

    def take_terms(d, carry):
        @pl.when(g + d < groups)
        def _():
            arrived(far_recv.at[d], r_tf.at[d], other(d))
            total[...] += far_recv[d].astype(F32)

        return carry

    lax.fori_loop(1, window + 1, take_terms, 0)
    for t in range(zs):
        for c in range(COLS):
            z_send[t, c * z_rows : (c + 1) * z_rows] = total[
                c * BLK + t * z_rows : c * BLK + (t + 1) * z_rows
            ].astype(BF16)
        z_send[t, COLS * z_rows :] = total[LAT + t * zp_rows : LAT + (t + 1) * zp_rows].astype(BF16)

    def z_copy(i):
        return remote(z_send.at[(hz + i) % zs], z_recv.at[i], s_z.at[i], r_z.at[i], deep(i))

    for i in range(1, zs):
        z_copy(i).start()

    for i in range(1, GRP):
        arrived(dq_recv.at[(j + GRP - i) % GRP], r_dq.at[i], mate(i))
    columns = []
    for h in range(GRP):
        columns += [dq_recv[h, :BLK], unpack_halves(dq_recv[h, BLK:])]
    dq_out[...] = jnp.concatenate(columns, axis=1)

    z_sum = z_send[hz].astype(F32)
    for i in range(1, zs):
        arrived(z_recv.at[i], r_z.at[i], deep(i))
        z_sum = z_sum + z_recv[i].astype(F32)
    z_fin[hz] = z_sum.astype(BF16)

    def zf_copy(i):
        return remote(z_fin.at[hz], z_fin.at[hz], s_zf.at[i], r_zf.at[i], deep(i))

    for i in range(1, zs):
        zf_copy(i).start()

    dw_sum[...] = dw_send[g].astype(F32)

    def take_dw(i, carry):
        arrived(dw_recv.at[i], r_dw.at[i], other(i))
        dw_sum[...] += dw_recv[i].astype(F32)
        return carry

    lax.fori_loop(1, groups, take_dw, 0)

    def dwf_copy(i):
        rows = pl.ds(pl.multiple_of((j + i) % GRP * o_rows, o_rows), o_rows)
        return remote(dw_sum.at[rows], dw_fin.at[j], s_dwf.at[i], r_dwf.at[i], mate(i))

    for i in range(1, GRP):
        dwf_copy(i).start()
    dw_fin[j] = dw_sum[pl.ds(pl.multiple_of(j * o_rows, o_rows), o_rows)]

    for i in range(1, zs):
        arrived(z_fin.at[(hz + zs - i) % zs], r_zf.at[i], deep(i))
    packed = []
    for t in range(zs):
        for c in range(COLS):
            part = z_fin[t, c * z_rows : (c + 1) * z_rows].astype(F32)
            dlat_out[t * z_rows : (t + 1) * z_rows, c * BLK : (c + 1) * BLK] = part
        packed.append(z_fin[t, COLS * z_rows :].astype(F32))
    packed = jnp.concatenate(packed, axis=0).T
    drope_out[...] = jnp.concatenate([packed[:ROPE], packed[ROPE:]], axis=1)

    for i in range(1, GRP):
        arrived(dw_fin.at[(j + GRP - i) % GRP], r_dwf.at[i], mate(i))
    dw_out[...] = jnp.concatenate([dw_fin[h] for h in range(GRP)], axis=1)

    for i in range(1, GRP):
        q_copy(i).wait_send()
        dq_copy(i).wait_send()
        dwf_copy(i).wait_send()
    for i in range(1, zs):
        z_copy(i).wait_send()
        zf_copy(i).wait_send()

    def end_blocks(d, carry):
        @pl.when((d > 0) & (g + d < groups))
        def _():
            far_copy(d).wait_send()

        @pl.when(g >= d)
        def _():
            own_copy(d).wait_send()
            near_copy(d).wait_send()
            pass_copy(d).wait_send()
            tc_copy(d).wait_send()
            tx_copy(d).wait_send()
            tn_copy(d).wait_send()

        @pl.when((d > 0) & (g >= d))
        def _():
            tf_copy(d).wait_send()

        return carry

    lax.fori_loop(0, window + 1, end_blocks, 0)

    def end_dw(i, carry):
        dw_copy(i).wait_send()
        return carry

    lax.fori_loop(1, groups, end_dw, 0)


def solution(mesh):
    groups = mesh.shape["ctx"] // GRP
    zs = mesh.shape["head"]
    span = min(groups - 1, (MOST + GRP - 2) // GRP) + 1
    w_rows = LAT // groups
    z_piece = PIECE // zs
    vmem = pltpu.VMEM
    dma = pltpu.SemaphoreType.DMA
    scratch = [
        vmem((GRP, ROWS, 128), BF16),
        vmem((GRP, ROWS, 128), BF16),
        vmem((span, GRP, PIECE, 128), BF16),
        vmem((span, 2, KEYS // 2, 256), BF16),
        vmem((LAT, 256), BF16),
        vmem((KEYS, 256), BF16),
        vmem((KEYS, 256), BF16),
        vmem((KEYS, VDIM), BF16),
        vmem((span, 2, GRP, HALF, KEYS), F32),
        vmem((span, 2, GRP, HALF, KEYS), F32),
        vmem((span, 1, KEYS), F32),
        vmem((span, 1, KEYS), F32),
        vmem((span, 1, KEYS), F32),
        vmem((span, 1, KEYS), F32),
        vmem((1, KEYS), F32),
        vmem((NOPE, KEYS), F32),
        vmem((ROPE, KEYS), F32),
        vmem((256, LAT), F32),
        vmem((span, GRP, PIECE, 128), BF16),
        vmem((span, 2, PIECE, 128), BF16),
        vmem((span, PIECE, 128), BF16),
        vmem((span, PIECE, 128), BF16),
        vmem((span, PIECE, 128), BF16),
        vmem((span, PIECE, 128), BF16),
        vmem((PIECE, 128), F32),
        vmem((groups, w_rows, 256), BF16),
        vmem((groups, w_rows, 256), BF16),
        vmem((w_rows, 256), F32),
        vmem((GRP, w_rows // GRP, 256), F32),
        vmem((GRP, BLK + HALF, 128), BF16),
        vmem((GRP, BLK + HALF, 128), BF16),
        vmem((zs, z_piece, 128), BF16),
        vmem((zs, z_piece, 128), BF16),
        vmem((zs, z_piece, 128), BF16),
    ]
    for count in (GRP, *[span] * 8, groups, GRP, GRP, zs, zs):
        scratch += [dma((count,)), dma((count,))]

    def local(query, latent, k_rope, d_out, w_kv, block_doc, block_order):
        whole = pl.BlockSpec(memory_space=pltpu.VMEM)
        scalars = pl.BlockSpec(memory_space=pltpu.SMEM)
        d_query, d_latent, d_rope, d_w_kv = pl.pallas_call(
            functools.partial(kernel, groups, zs),
            out_shape=(
                jax.ShapeDtypeStruct(query.shape, BF16),
                jax.ShapeDtypeStruct((BLK, LAT), F32),
                jax.ShapeDtypeStruct((ROPE, BLK), F32),
                jax.ShapeDtypeStruct((w_rows // GRP, GRP * 256), F32),
            ),
            in_specs=[whole] * 5 + [scalars] * 2,
            out_specs=(whole,) * 4,
            scratch_shapes=scratch,
            compiler_params=pltpu.CompilerParams(
                collective_id=0, has_side_effects=True, vmem_limit_bytes=56 * 1024 * 1024
            ),
        )(query, latent, k_rope.T, d_out, w_kv, block_doc, block_order)
        return d_query, d_latent, d_rope.T, d_w_kv

    return jax.shard_map(
        local,
        mesh=mesh,
        in_specs=(
            P("ctx", "head"),
            P("ctx", None),
            P("ctx", None),
            P("ctx", "head"),
            P(None, "head"),
            P(),
            P(),
        ),
        out_specs=(P("ctx", "head"), P("ctx", None), P("ctx", None), P("ctx", "head")),
        check_vma=False,
    )
```

```python
import functools
import math

import jax
import jax.numpy as jnp
from jax import lax
from jax.experimental import pallas as pl
from jax.experimental.pallas import tpu as pltpu
from jax.sharding import PartitionSpec as P

LAT = 512
ROPE = 64
NOPE = 128
VDIM = 128
BLK = 128
HEAD = NOPE + ROPE
HALF = BLK // 2
SIDE = 4
GRP = 4
KEYS = GRP * BLK
ROWS = 2 * BLK + HALF
COLS = LAT // BLK
PIECE = LAT + HALF
PASS_LAG, TILE_LAG = 3, 5
CHIP_LAG, SLOT_LAG = 1, 4
MOST = 36
SCALE = HEAD**-0.5
LOG2E = math.log2(math.e)
NEG = -1e30
MESH = pl.DeviceIdType.MESH
F32 = jnp.float32
BF16 = jnp.bfloat16


def nt(a, b):
    return lax.dot_general(a, b, (((1,), (1,)), ((), ())), preferred_element_type=F32)


def tn(a, b):
    return lax.dot_general(a, b, (((0,), (0,)), ((), ())), preferred_element_type=F32)


def nn(a, b):
    return jnp.dot(a, b, preferred_element_type=F32)


def pack_halves(rows):
    return jnp.concatenate([rows[:HALF], rows[HALF:]], axis=1)


def unpack_halves(rows):
    return jnp.concatenate([rows[:, :ROPE], rows[:, ROPE:]], axis=0)


def kernel(
    groups,
    zs,
    query,
    latent,
    k_rope,
    d_out,
    w_kv,
    doc,
    order,
    dq_out,
    dlat_out,
    drope_out,
    dw_out,
    q_stage,
    q_buf,
    lat_buf,
    k_buf,
    w_head,
    q_lo,
    q_hi,
    g_out,
    p_buf,
    dp_buf,
    m_ref,
    mass_ref,
    ws_ref,
    fac_ref,
    delta_ref,
    dqn,
    dqr,
    dw_acc,
    terms,
    core_recv,
    near_send,
    near_recv,
    far_send,
    far_recv,
    up_send,
    up_recv,
    total,
    dw_send,
    dw_recv,
    dw_sum,
    dw_fin,
    dq_send,
    dq_recv,
    z_send,
    z_recv,
    z_fin,
    s_q,
    r_q,
    s_down,
    s_fan,
    s_corner,
    r_far,
    s_own,
    r_own,
    s_near,
    r_near,
    s_pass,
    r_pass,
    s_tc,
    r_tc,
    s_tx,
    r_tx,
    s_tn,
    r_tn,
    s_tf,
    r_tf,
    s_up,
    r_up,
    s_dw,
    r_dw,
    s_dwf,
    r_dwf,
    s_dq,
    r_dq,
    s_z,
    r_z,
    s_zf,
    r_zf,
):
    ctx = lax.axis_index("ctx")
    hz = lax.axis_index("head")
    g = ctx // GRP
    j = ctx % GRP
    z_lo = j // 2
    core = j % 2
    j_core = 2 * z_lo + 1 - core
    j_near = 2 * (1 - z_lo) + core
    j_next = 2 * (1 - z_lo) + 1 - core
    window = min(groups - 1, (MOST + GRP - 2) // GRP)
    y = g // SIDE
    x = g % SIDE
    w_rows = LAT // groups
    o_rows = w_rows // GRP
    z_rows = BLK // zs
    zp_rows = HALF // zs

    def mate(i):
        return ((g * GRP + (j + i) % GRP), hz)

    def other(i):
        return (((g + i) % groups) * GRP + j, hz)

    def deep(i):
        return (ctx, (hz + i) % zs)

    beside = (g * GRP + j_core, hz)
    ahead = (g * GRP + j_near, (hz + z_lo + core * (zs - 1)) % zs)
    behind = (g * GRP + j_near, (hz + z_lo + (1 - core) * (zs - 1)) % zs)

    def remote(src, dst, send, recv, to):
        return pltpu.make_async_remote_copy(
            src_ref=src, dst_ref=dst, send_sem=send, recv_sem=recv, device_id=to, device_id_type=MESH
        )

    def arrived(ref, sem, to):
        remote(ref, ref, sem, sem, to).wait_recv()

    barrier = pltpu.get_barrier_semaphore()
    for i in range(1, GRP):
        pl.semaphore_signal(barrier, inc=1, device_id=mate(i), device_id_type=MESH)
    for i in range(1, zs):
        pl.semaphore_signal(barrier, inc=1, device_id=deep(i), device_id_type=MESH)
    pl.semaphore_signal(barrier, inc=1, device_id=ahead, device_id_type=MESH)
    pl.semaphore_signal(barrier, inc=1, device_id=behind, device_id_type=MESH)

    def greet(i, carry):
        pl.semaphore_signal(barrier, inc=1, device_id=other(i), device_id_type=MESH)
        return carry

    lax.fori_loop(1, groups, greet, 0)

    for c in range(COLS):
        lat_buf[0, j, c * BLK : (c + 1) * BLK] = latent[:, c * BLK : (c + 1) * BLK]
    lat_buf[0, j, LAT:] = pack_halves(k_rope[...].astype(F32).T.astype(BF16))
    for h in range(GRP):
        q_stage[h, :BLK] = query[:, HEAD * h : HEAD * h + NOPE]
        q_stage[h, BLK : 2 * BLK] = d_out[:, VDIM * h : VDIM * h + VDIM]
        q_stage[h, 2 * BLK :] = pack_halves(query[:, HEAD * h + NOPE : HEAD * h + HEAD])

    pl.semaphore_wait(barrier, GRP - 1 + zs - 1 + 2 + groups - 1)

    def row_mate(i):
        return ((g - x + (x + i) % SIDE) * GRP + j, hz)

    def down_copy(dy):
        here, there = SIDE * dy, SIDE * (dy + 1)
        to = ((g + SIDE) * GRP + j, hz)
        return remote(lat_buf.at[here, j], lat_buf.at[there, j], s_down.at[dy], r_far.at[there], to)

    def fan_copy(dy, i):
        d = SIDE * dy + (x + i) % SIDE - x
        return remote(lat_buf.at[SIDE * dy, j], lat_buf.at[d, j], s_fan.at[dy, i], r_far.at[d], row_mate(i))

    def in_fan(dy, i):
        d = SIDE * dy + (x + i) % SIDE - x
        return (y >= dy) & (d >= 1) & (d <= window)

    corner_out = (y == 0) & (x == SIDE - 1)

    def corner_copy():
        return remote(lat_buf.at[0, j], lat_buf.at[window, j], s_corner.at[0], r_far.at[window], other(window))

    def fan(dy):
        for i in (1, 3, 2):

            @pl.when(in_fan(dy, i))
            def _():
                fan_copy(dy, i).start()

    def own_copy(d):
        return remote(lat_buf.at[d, j], lat_buf.at[d, j], s_own.at[d], r_own.at[d], beside)

    def near_copy(d):
        return remote(lat_buf.at[d, j], lat_buf.at[d, j], s_near.at[d], r_near.at[d], ahead)

    def pass_copy(d):
        return remote(lat_buf.at[d, j_near], lat_buf.at[d, j_near], s_pass.at[d], r_pass.at[d], beside)

    def q_copy(i):
        return remote(q_stage.at[(j + i) % GRP], q_buf.at[j], s_q.at[i], r_q.at[i], mate(i))

    near_copy(0).start()
    own_copy(0).start()

    @pl.when(y + 1 < SIDE)
    def _():
        down_copy(0).start()

    fan(0)

    @pl.when(corner_out)
    def _():
        corner_copy().start()

    for i in range(1, GRP):
        q_copy(i).start()
    q_buf[j] = q_stage[j]
    w_head[...] = w_kv[:, pl.ds(pl.multiple_of(j * 256, 256), 256)]

    slot_of = lax.broadcasted_iota(jnp.int32, (1, KEYS), 1) // BLK
    in_slot = lax.broadcasted_iota(jnp.int32, (1, KEYS), 1) % BLK
    q_pos = jnp.zeros((1, KEYS), jnp.int32)
    q_doc = jnp.zeros((1, KEYS), jnp.int32)
    for s in range(GRP):
        block = order[GRP * g + s]
        q_pos = jnp.where(slot_of == s, block * BLK + in_slot, q_pos)
        q_doc = jnp.where(slot_of == s, doc[block], q_doc)

    m_ref[...] = jnp.full(m_ref.shape, NEG, F32)
    mass_ref[...] = jnp.zeros(mass_ref.shape, F32)
    ws_ref[...] = jnp.zeros(ws_ref.shape, F32)

    def latents_of(d):
        return jnp.concatenate(
            [
                jnp.concatenate([lat_buf[d, s, c * BLK : (c + 1) * BLK] for c in range(COLS)], axis=1)
                for s in range(GRP)
            ],
            axis=0,
        )

    def half_rows(rows, half):
        return jnp.concatenate(
            [rows[s * BLK + half * HALF : s * BLK + half * HALF + HALF] for s in range(GRP)], axis=0
        )

    def scores_tile(d, local):
        kv = nn(latents_of(d), w_head[...]).astype(BF16)
        rope = jnp.concatenate([lat_buf[d, s, LAT:] for s in range(GRP)], axis=0)
        top = jnp.full((8, KEYS), NEG, F32)
        for half in range(2):
            k_buf[d, half] = jnp.concatenate([half_rows(kv[:, :NOPE], half), rope], axis=1)
            scores = nt(k_buf[d, half], (q_lo, q_hi)[half][...])
            for s in range(GRP):
                block = order[GRP * (g - d) + s]
                same = q_doc == doc[block]
                part = scores[s * HALF : s * HALF + HALF] * (SCALE * LOG2E)
                if local:
                    pos = lax.broadcasted_iota(jnp.int32, (HALF, 1), 0) + (block * BLK + half * HALF)
                    part = jnp.where(same & (pos <= q_pos), part, NEG)
                else:
                    part = part + jnp.where(same, 0.0, NEG)
                p_buf[d, half, s] = part
                top = jnp.maximum(top, jnp.max(part.reshape(HALF // 8, 8, KEYS), axis=0))
        peak = jnp.max(top, axis=0, keepdims=True)
        mass = jnp.zeros((8, KEYS), F32)
        weighted = jnp.zeros((8, KEYS), F32)
        for half in range(2):
            dp = nt(half_rows(kv[:, NOPE:], half), g_out[...])
            for s in range(GRP):
                here = dp[s * HALF : s * HALF + HALF]
                p = jnp.exp2(p_buf[d, half, s] - peak)
                p_buf[d, half, s] = p
                dp_buf[d, half, s] = here
                mass = mass + jnp.sum(p.reshape(HALF // 8, 8, KEYS), axis=0)
                weighted = weighted + jnp.sum((p * here).reshape(HALF // 8, 8, KEYS), axis=0)
        m_ref[d] = peak
        mass_ref[d] = jnp.sum(mass, axis=0, keepdims=True)
        ws_ref[d] = jnp.sum(weighted, axis=0, keepdims=True)

    def spread(d):
        @pl.when((d <= window) & (g >= d) & (d % SIDE != 0))
        def _():
            arrived(lat_buf.at[d, j], r_far.at[d], beside)
            near_copy(d).start()
            own_copy(d).start()

    def hand_on(d):
        @pl.when((d >= 0) & (d <= window) & (g >= d))
        def _():
            arrived(lat_buf.at[d, j_near], r_near.at[d], beside)
            pass_copy(d).start()

    def whole(d):
        arrived(lat_buf.at[d, j_core], r_own.at[d], beside)
        arrived(lat_buf.at[d, j_next], r_pass.at[d], beside)

    hand_on(0)

    @pl.when(y >= 1)
    def _():
        arrived(lat_buf.at[SIDE, j], r_far.at[SIDE], beside)

        @pl.when(y + 1 < SIDE)
        def _():
            down_copy(1).start()

        near_copy(SIDE).start()
        own_copy(SIDE).start()

    fan(1)
    for i in range(1, GRP):
        arrived(q_buf.at[(j + GRP - i) % GRP], r_q.at[i], mate(i))
    blank = jnp.zeros((HALF, ROPE), BF16)
    for s in range(GRP):
        at = s * BLK
        pair = q_buf[s, 2 * BLK :]
        first, second = pair[:, :ROPE], pair[:, ROPE:]
        q_lo[at : at + BLK, :NOPE] = q_buf[s, :BLK]
        q_hi[at : at + BLK, :NOPE] = q_buf[s, :BLK]
        g_out[at : at + BLK] = q_buf[s, BLK : 2 * BLK]
        q_lo[at : at + HALF, NOPE:] = jnp.concatenate([first, blank], axis=1)
        q_lo[at + HALF : at + BLK, NOPE:] = jnp.concatenate([second, blank], axis=1)
        q_hi[at : at + HALF, NOPE:] = jnp.concatenate([blank, first], axis=1)
        q_hi[at + HALF : at + BLK, NOPE:] = jnp.concatenate([blank, second], axis=1)
    whole(0)
    scores_tile(0, True)

    @pl.when(y >= 2)
    def _():
        arrived(lat_buf.at[2 * SIDE, j], r_far.at[2 * SIDE], beside)
        near_copy(2 * SIDE).start()
        own_copy(2 * SIDE).start()

    fan(2)

    def far_scores(i, carry):
        spread(i)

        @pl.when(i > PASS_LAG)
        def _():
            hand_on(i - PASS_LAG)

        @pl.when((i > TILE_LAG) & (g >= i - TILE_LAG))
        def _():
            whole(i - TILE_LAG)
            scores_tile(i - TILE_LAG, False)

        return carry

    lax.fori_loop(1, window + TILE_LAG + 1, far_scores, 0)

    peak = jnp.max(m_ref[...], axis=0)
    factors = jnp.exp2(m_ref[...] - peak[None])
    mass = jnp.sum(mass_ref[...] * factors, axis=0)
    weighted = jnp.sum(ws_ref[...] * factors, axis=0)
    fac_ref[...] = factors / mass[None]
    delta_ref[...] = weighted / mass
    dqn[...] = jnp.zeros(dqn.shape, F32)
    dqr[...] = jnp.zeros(dqr.shape, F32)
    dw_acc[...] = jnp.zeros(dw_acc.shape, F32)

    def grads_tile(d):
        factor = fac_ref[d]
        delta = delta_ref[...]
        rope_sum = None
        pairs = []
        for half in range(2):
            mixed, probs = [], []
            for s in range(GRP):
                p = p_buf[d, half, s] * factor
                mixed.append((p * (dp_buf[d, half, s] - delta)).astype(BF16))
                probs.append(p.astype(BF16))
            mixed = jnp.concatenate(mixed, axis=0)
            probs = jnp.concatenate(probs, axis=0)
            d_keys = nn(mixed, (q_lo, q_hi)[half][...]) * SCALE
            d_values = nn(probs, g_out[...])
            rope_sum = d_keys[:, NOPE:] if half == 0 else rope_sum + d_keys[:, NOPE:]
            pairs.append(jnp.concatenate([d_keys[:, :NOPE], d_values], axis=1).astype(BF16))
            dq = tn(k_buf[d, half], mixed)
            dqn[...] += dq[:NOPE]
            dqr[...] += dq[NOPE + half * ROPE : NOPE + half * ROPE + ROPE]
        pairs = jnp.concatenate(
            [pairs[half][s * HALF : s * HALF + HALF] for s in range(GRP) for half in range(2)], axis=0
        )
        d_lat = nt(pairs, w_head[...])
        for s in range(GRP):
            for c in range(COLS):
                part = d_lat[s * BLK : (s + 1) * BLK, c * BLK : (c + 1) * BLK]
                terms[d, s, c * BLK : (c + 1) * BLK] = part.astype(BF16)
            terms[d, s, LAT:] = rope_sum[s * HALF : s * HALF + HALF].astype(BF16)
        dw_acc[...] += tn(pairs, latents_of(d))

    def tc_copy(d):
        return remote(terms.at[d, j_core], core_recv.at[d, 0], s_tc.at[d], r_tc.at[d], beside)

    def tx_copy(d):
        return remote(terms.at[d, j_next], core_recv.at[d, 1], s_tx.at[d], r_tx.at[d], beside)

    def tn_copy(d):
        return remote(near_send.at[d], near_recv.at[d], s_tn.at[d], r_tn.at[d], behind)

    def tf_copy(d):
        return remote(far_send.at[d], far_recv.at[d], s_tf.at[d], r_tf.at[d], row_mate(4 * SIDE - d))

    def tf_corner():
        d = window
        return remote(far_send.at[d], far_recv.at[d], s_tf.at[d], r_tf.at[d], other(groups - d))

    def up_copy(dy):
        to = ((g - SIDE) * GRP + j, hz)
        return remote(up_send.at[dy], up_recv.at[dy], s_up.at[dy], r_up.at[dy], to)

    def chip_sum(d):
        @pl.when((d <= window) & (g >= d))
        def _():
            arrived(core_recv.at[d, 1], r_tx.at[d], beside)
            near_send[d] = (terms[d, j_near].astype(F32) + core_recv[d, 1].astype(F32)).astype(BF16)
            tn_copy(d).start()

    def slot_sum(d):
        arrived(core_recv.at[d, 0], r_tc.at[d], beside)
        arrived(near_recv.at[d], r_tn.at[d], beside)
        return terms[d, j].astype(F32) + core_recv[d, 0].astype(F32) + near_recv[d].astype(F32)

    def send_terms(d):
        @pl.when((d <= window) & (g >= d))
        def _():
            far_send[d] = slot_sum(d).astype(BF16)

            @pl.when((d % SIDE != 0) & ((d < window) | (x > 0)))
            def _():
                tf_copy(d).start()

            @pl.when((d == window) & (x == 0))
            def _():
                tf_corner().start()

    def far_grads(step, carry):
        d = window - step

        @pl.when(g >= d)
        def _():
            grads_tile(d)
            tx_copy(d).start()
            tc_copy(d).start()

        chip_sum(d + CHIP_LAG)
        send_terms(d + SLOT_LAG)
        return carry

    lax.fori_loop(0, window + 1, far_grads, 0)
    for d in range(CHIP_LAG - 1, -1, -1):
        chip_sum(d)

    dq_nope = (dqn[...] * SCALE).T.astype(BF16)
    dq_rope = (dqr[...] * SCALE).T.astype(BF16)
    for s in range(GRP):
        dq_send[s, :BLK] = dq_nope[s * BLK : s * BLK + BLK]
        dq_send[s, BLK:] = pack_halves(dq_rope[s * BLK : s * BLK + BLK])
    dq_recv[j] = dq_send[j]

    def dq_copy(i):
        return remote(dq_send.at[(j + i) % GRP], dq_recv.at[j], s_dq.at[i], r_dq.at[i], mate(i))

    for i in range(1, GRP):
        dq_copy(i).start()

    def add(ref, sem):
        arrived(ref, sem, beside)
        total[...] += ref[...].astype(F32)

    def row_sum(dy):
        for i in (1, 3, 2):
            d = SIDE * dy + (x + i) % SIDE - x

            @pl.when((d >= 1) & (d <= window))
            def _():
                add(far_recv.at[d], r_tf.at[d])

    for d in range(SLOT_LAG - 1, 3, -1):
        send_terms(d)

    @pl.when(y >= 2)
    def _():
        total[...] = far_send[2 * SIDE].astype(F32)
        row_sum(2)
        up_send[1] = total[...].astype(BF16)
        up_copy(1).start()

    for d in range(min(SLOT_LAG - 1, 3), 0, -1):
        send_terms(d)

    @pl.when(y >= 1)
    def _():
        total[...] = far_send[SIDE].astype(F32)
        row_sum(1)

        @pl.when(y + 1 < SIDE)
        def _():
            add(up_recv.at[1], r_up.at[1])

        up_send[0] = total[...].astype(BF16)
        up_copy(0).start()

    grad_w = dw_acc[...].T.astype(BF16)
    for i in range(groups):
        dw_send[i] = grad_w[i * w_rows : (i + 1) * w_rows]

    def dw_copy(i):
        return remote(dw_send.at[(g + i) % groups], dw_recv.at[i], s_dw.at[i], r_dw.at[i], other(i))

    def send_dw(i, carry):
        dw_copy(i).start()
        return carry

    lax.fori_loop(1, groups, send_dw, 0)

    total[...] = slot_sum(0)
    row_sum(0)

    @pl.when(corner_out)
    def _():
        add(far_recv.at[window], r_tf.at[window])

    @pl.when(y + 1 < SIDE)
    def _():
        add(up_recv.at[0], r_up.at[0])

    for t in range(zs):
        for c in range(COLS):
            z_send[t, c * z_rows : (c + 1) * z_rows] = total[
                c * BLK + t * z_rows : c * BLK + (t + 1) * z_rows
            ].astype(BF16)
        z_send[t, COLS * z_rows :] = total[LAT + t * zp_rows : LAT + (t + 1) * zp_rows].astype(BF16)

    def z_copy(i):
        return remote(z_send.at[(hz + i) % zs], z_recv.at[i], s_z.at[i], r_z.at[i], deep(i))

    for i in range(1, zs):
        z_copy(i).start()

    for i in range(1, GRP):
        arrived(dq_recv.at[(j + GRP - i) % GRP], r_dq.at[i], mate(i))
    columns = []
    for h in range(GRP):
        columns += [dq_recv[h, :BLK], unpack_halves(dq_recv[h, BLK:])]
    dq_out[...] = jnp.concatenate(columns, axis=1)

    z_sum = z_send[hz].astype(F32)
    for i in range(1, zs):
        arrived(z_recv.at[i], r_z.at[i], deep(i))
        z_sum = z_sum + z_recv[i].astype(F32)
    z_fin[hz] = z_sum.astype(BF16)

    def zf_copy(i):
        return remote(z_fin.at[hz], z_fin.at[hz], s_zf.at[i], r_zf.at[i], deep(i))

    for i in range(1, zs):
        zf_copy(i).start()

    dw_sum[...] = dw_send[g].astype(F32)

    def take_dw(i, carry):
        arrived(dw_recv.at[i], r_dw.at[i], other(i))
        dw_sum[...] += dw_recv[i].astype(F32)
        return carry

    lax.fori_loop(1, groups, take_dw, 0)

    def dwf_copy(i):
        rows = pl.ds(pl.multiple_of((j + i) % GRP * o_rows, o_rows), o_rows)
        return remote(dw_sum.at[rows], dw_fin.at[j], s_dwf.at[i], r_dwf.at[i], mate(i))

    for i in range(1, GRP):
        dwf_copy(i).start()
    dw_fin[j] = dw_sum[pl.ds(pl.multiple_of(j * o_rows, o_rows), o_rows)]

    for i in range(1, zs):
        arrived(z_fin.at[(hz + zs - i) % zs], r_zf.at[i], deep(i))
    packed = []
    for t in range(zs):
        for c in range(COLS):
            part = z_fin[t, c * z_rows : (c + 1) * z_rows].astype(F32)
            dlat_out[t * z_rows : (t + 1) * z_rows, c * BLK : (c + 1) * BLK] = part
        packed.append(z_fin[t, COLS * z_rows :].astype(F32))
    packed = jnp.concatenate(packed, axis=0).T
    drope_out[...] = jnp.concatenate([packed[:ROPE], packed[ROPE:]], axis=1)

    for i in range(1, GRP):
        arrived(dw_fin.at[(j + GRP - i) % GRP], r_dwf.at[i], mate(i))
    dw_out[...] = jnp.concatenate([dw_fin[h] for h in range(GRP)], axis=1)

    for i in range(1, GRP):
        q_copy(i).wait_send()
        dq_copy(i).wait_send()
        dwf_copy(i).wait_send()
    for i in range(1, zs):
        z_copy(i).wait_send()
        zf_copy(i).wait_send()

    def end_blocks(d, carry):
        @pl.when(g >= d)
        def _():
            own_copy(d).wait_send()
            near_copy(d).wait_send()
            pass_copy(d).wait_send()
            tc_copy(d).wait_send()
            tx_copy(d).wait_send()
            tn_copy(d).wait_send()

        @pl.when((d % SIDE != 0) & (g >= d))
        def _():
            tf_copy(d).wait_send()

        return carry

    lax.fori_loop(0, window + 1, end_blocks, 0)
    for dy in range(2):

        @pl.when((y + 1 < SIDE) & (y >= dy))
        def _():
            down_copy(dy).wait_send()

        @pl.when(y > dy)
        def _():
            up_copy(dy).wait_send()

    for dy in range(3):
        for i in (1, 3, 2):

            @pl.when(in_fan(dy, i))
            def _():
                fan_copy(dy, i).wait_send()

    @pl.when(corner_out)
    def _():
        corner_copy().wait_send()


    def end_dw(i, carry):
        dw_copy(i).wait_send()
        return carry

    lax.fori_loop(1, groups, end_dw, 0)


def solution(mesh):
    groups = mesh.shape["ctx"] // GRP
    zs = mesh.shape["head"]
    span = min(groups - 1, (MOST + GRP - 2) // GRP) + 1
    w_rows = LAT // groups
    z_piece = PIECE // zs
    vmem = pltpu.VMEM
    dma = pltpu.SemaphoreType.DMA
    scratch = [
        vmem((GRP, ROWS, 128), BF16),
        vmem((GRP, ROWS, 128), BF16),
        vmem((span, GRP, PIECE, 128), BF16),
        vmem((span, 2, KEYS // 2, 256), BF16),
        vmem((LAT, 256), BF16),
        vmem((KEYS, 256), BF16),
        vmem((KEYS, 256), BF16),
        vmem((KEYS, VDIM), BF16),
        vmem((span, 2, GRP, HALF, KEYS), F32),
        vmem((span, 2, GRP, HALF, KEYS), F32),
        vmem((span, 1, KEYS), F32),
        vmem((span, 1, KEYS), F32),
        vmem((span, 1, KEYS), F32),
        vmem((span, 1, KEYS), F32),
        vmem((1, KEYS), F32),
        vmem((NOPE, KEYS), F32),
        vmem((ROPE, KEYS), F32),
        vmem((256, LAT), F32),
        vmem((span, GRP, PIECE, 128), BF16),
        vmem((span, 2, PIECE, 128), BF16),
        vmem((span, PIECE, 128), BF16),
        vmem((span, PIECE, 128), BF16),
        vmem((span, PIECE, 128), BF16),
        vmem((span, PIECE, 128), BF16),
        vmem((2, PIECE, 128), BF16),
        vmem((2, PIECE, 128), BF16),
        vmem((PIECE, 128), F32),
        vmem((groups, w_rows, 256), BF16),
        vmem((groups, w_rows, 256), BF16),
        vmem((w_rows, 256), F32),
        vmem((GRP, w_rows // GRP, 256), F32),
        vmem((GRP, BLK + HALF, 128), BF16),
        vmem((GRP, BLK + HALF, 128), BF16),
        vmem((zs, z_piece, 128), BF16),
        vmem((zs, z_piece, 128), BF16),
        vmem((zs, z_piece, 128), BF16),
    ]
    scratch += [dma((GRP,)), dma((GRP,)), dma((2,)), dma((3, SIDE)), dma((1,)), dma((span,))]
    for count in (*[span] * 7, 2, groups, GRP, GRP, zs, zs):
        scratch += [dma((count,)), dma((count,))]

    def local(query, latent, k_rope, d_out, w_kv, block_doc, block_order):
        whole = pl.BlockSpec(memory_space=pltpu.VMEM)
        scalars = pl.BlockSpec(memory_space=pltpu.SMEM)
        d_query, d_latent, d_rope, d_w_kv = pl.pallas_call(
            functools.partial(kernel, groups, zs),
            out_shape=(
                jax.ShapeDtypeStruct(query.shape, BF16),
                jax.ShapeDtypeStruct((BLK, LAT), F32),
                jax.ShapeDtypeStruct((ROPE, BLK), F32),
                jax.ShapeDtypeStruct((w_rows // GRP, GRP * 256), F32),
            ),
            in_specs=[whole] * 5 + [scalars] * 2,
            out_specs=(whole,) * 4,
            scratch_shapes=scratch,
            compiler_params=pltpu.CompilerParams(
                collective_id=0, has_side_effects=True, vmem_limit_bytes=56 * 1024 * 1024
            ),
        )(query, latent, k_rope.T, d_out, w_kv, block_doc, block_order)
        return d_query, d_latent, d_rope.T, d_w_kv

    return jax.shard_map(
        local,
        mesh=mesh,
        in_specs=(
            P("ctx", "head"),
            P("ctx", None),
            P("ctx", None),
            P("ctx", "head"),
            P(None, "head"),
            P(),
            P(),
        ),
        out_specs=(P("ctx", "head"), P("ctx", None), P("ctx", None), P("ctx", "head")),
        check_vma=False,
    )
```

```python
import functools
import math

import jax
import jax.numpy as jnp
from jax import lax
from jax.experimental import pallas as pl
from jax.experimental.pallas import tpu as pltpu
from jax.sharding import PartitionSpec as P

LAT = 512
ROPE = 64
NOPE = 128
VDIM = 128
BLK = 128
HEAD = NOPE + ROPE
HALF = BLK // 2
SIDE = 4
GRP = 4
KEYS = GRP * BLK
ROWS = 2 * BLK + HALF
COLS = LAT // BLK
PIECE = LAT + HALF
PASS_LAG, TILE_LAG = 3, 5
CHIP_LAG, SLOT_LAG = 1, 4
MOST = 36
SCALE = HEAD**-0.5
LOG2E = math.log2(math.e)
NEG = -1e30
MESH = pl.DeviceIdType.MESH
F32 = jnp.float32
BF16 = jnp.bfloat16


def nt(a, b):
    return lax.dot_general(a, b, (((1,), (1,)), ((), ())), preferred_element_type=F32)


def tn(a, b):
    return lax.dot_general(a, b, (((0,), (0,)), ((), ())), preferred_element_type=F32)


def nn(a, b):
    return jnp.dot(a, b, preferred_element_type=F32)


def pack_halves(rows):
    return jnp.concatenate([rows[:HALF], rows[HALF:]], axis=1)


def unpack_halves(rows):
    return jnp.concatenate([rows[:, :ROPE], rows[:, ROPE:]], axis=0)


def keep(a, b, c, d, a_out, b_out, c_out, d_out):
    for src, dst in ((a, a_out), (b, b_out), (c, c_out), (d, d_out)):
        dst[...] = src[...]


def kernel(
    groups,
    zs,
    query,
    latent,
    k_rope,
    d_out,
    w_kv,
    doc,
    order,
    dq_out,
    dlat_out,
    drope_out,
    dw_out,
    q_stage,
    q_buf,
    lat_buf,
    k_buf,
    w_head,
    q_lo,
    q_hi,
    g_out,
    p_buf,
    dp_buf,
    m_ref,
    mass_ref,
    ws_ref,
    fac_ref,
    delta_ref,
    dqn,
    dqr,
    dw_acc,
    terms,
    core_recv,
    near_send,
    near_recv,
    far_send,
    far_recv,
    up_send,
    up_recv,
    total,
    dw_send,
    dw_recv,
    dw_sum,
    dw_fin,
    dq_send,
    dq_recv,
    z_send,
    z_recv,
    z_fin,
    s_w,
    s_q,
    r_q,
    s_down,
    s_fan,
    s_corner,
    r_far,
    s_own,
    r_own,
    s_near,
    r_near,
    s_pass,
    r_pass,
    s_tc,
    r_tc,
    s_tx,
    r_tx,
    s_tn,
    r_tn,
    s_tf,
    r_tf,
    s_up,
    r_up,
    s_dw,
    r_dw,
    s_dwf,
    r_dwf,
    s_dq,
    r_dq,
    s_z,
    r_z,
    s_zf,
    r_zf,
):
    ctx = lax.axis_index("ctx")
    hz = lax.axis_index("head")
    g = ctx // GRP
    j = ctx % GRP
    z_lo = j // 2
    core = j % 2
    j_core = 2 * z_lo + 1 - core
    j_near = 2 * (1 - z_lo) + core
    j_next = 2 * (1 - z_lo) + 1 - core
    window = min(groups - 1, (MOST + GRP - 2) // GRP)
    y = g // SIDE
    x = g % SIDE
    w_rows = LAT // groups
    o_rows = w_rows // GRP
    z_rows = BLK // zs
    zp_rows = HALF // zs

    def mate(i):
        return ((g * GRP + (j + i) % GRP), hz)

    def other(i):
        return (((g + i) % groups) * GRP + j, hz)

    def deep(i):
        return (ctx, (hz + i) % zs)

    beside = (g * GRP + j_core, hz)
    ahead = (g * GRP + j_near, (hz + z_lo + core * (zs - 1)) % zs)
    behind = (g * GRP + j_near, (hz + z_lo + (1 - core) * (zs - 1)) % zs)

    def remote(src, dst, send, recv, to):
        return pltpu.make_async_remote_copy(
            src_ref=src, dst_ref=dst, send_sem=send, recv_sem=recv, device_id=to, device_id_type=MESH
        )

    def arrived(ref, sem, to):
        remote(ref, ref, sem, sem, to).wait_recv()

    columns = pl.ds(pl.multiple_of(j * 256, 256), 256)
    weights = pltpu.make_async_copy(w_kv.at[:, columns], w_head, s_w.at[0])
    weights.start()
    barrier = pltpu.get_barrier_semaphore()
    for i in range(1, GRP):
        pl.semaphore_signal(barrier, inc=1, device_id=mate(i), device_id_type=MESH)
    for i in range(1, zs):
        pl.semaphore_signal(barrier, inc=1, device_id=deep(i), device_id_type=MESH)
    pl.semaphore_signal(barrier, inc=1, device_id=ahead, device_id_type=MESH)
    pl.semaphore_signal(barrier, inc=1, device_id=behind, device_id_type=MESH)

    def greet(i, carry):
        pl.semaphore_signal(barrier, inc=1, device_id=other(i), device_id_type=MESH)
        return carry

    lax.fori_loop(1, groups, greet, 0)

    for c in range(COLS):
        lat_buf[0, j, c * BLK : (c + 1) * BLK] = latent[:, c * BLK : (c + 1) * BLK]
    lat_buf[0, j, LAT:] = pack_halves(k_rope[...].astype(F32).T.astype(BF16))
    for h in range(GRP):
        q_stage[h, :BLK] = query[:, HEAD * h : HEAD * h + NOPE]
        q_stage[h, BLK : 2 * BLK] = d_out[:, VDIM * h : VDIM * h + VDIM]
        q_stage[h, 2 * BLK :] = pack_halves(query[:, HEAD * h + NOPE : HEAD * h + HEAD])

    pl.semaphore_wait(barrier, GRP - 1 + zs - 1 + 2 + groups - 1)

    def row_mate(i):
        return ((g - x + (x + i) % SIDE) * GRP + j, hz)

    def down_copy(dy):
        here, there = SIDE * dy, SIDE * (dy + 1)
        to = ((g + SIDE) * GRP + j, hz)
        return remote(lat_buf.at[here, j], lat_buf.at[there, j], s_down.at[dy], r_far.at[there], to)

    def fan_copy(dy, i):
        d = SIDE * dy + (x + i) % SIDE - x
        return remote(lat_buf.at[SIDE * dy, j], lat_buf.at[d, j], s_fan.at[dy, i], r_far.at[d], row_mate(i))

    def in_fan(dy, i):
        d = SIDE * dy + (x + i) % SIDE - x
        return (y >= dy) & (d >= 1) & (d <= window)

    corner_out = (y == 0) & (x == SIDE - 1)

    def corner_copy():
        return remote(lat_buf.at[0, j], lat_buf.at[window, j], s_corner.at[0], r_far.at[window], other(window))

    def fan(dy):
        for i in (1, 3, 2):

            @pl.when(in_fan(dy, i))
            def _():
                fan_copy(dy, i).start()

    def own_copy(d):
        return remote(lat_buf.at[d, j], lat_buf.at[d, j], s_own.at[d], r_own.at[d], beside)

    def near_copy(d):
        return remote(lat_buf.at[d, j], lat_buf.at[d, j], s_near.at[d], r_near.at[d], ahead)

    def pass_copy(d):
        return remote(lat_buf.at[d, j_near], lat_buf.at[d, j_near], s_pass.at[d], r_pass.at[d], beside)

    def q_copy(i):
        return remote(q_stage.at[(j + i) % GRP], q_buf.at[j], s_q.at[i], r_q.at[i], mate(i))

    near_copy(0).start()
    own_copy(0).start()

    @pl.when(y + 1 < SIDE)
    def _():
        down_copy(0).start()

    fan(0)

    @pl.when(corner_out)
    def _():
        corner_copy().start()

    for i in range(1, GRP):
        q_copy(i).start()
    q_buf[j] = q_stage[j]

    slot_of = lax.broadcasted_iota(jnp.int32, (1, KEYS), 1) // BLK
    in_slot = lax.broadcasted_iota(jnp.int32, (1, KEYS), 1) % BLK
    q_pos = jnp.zeros((1, KEYS), jnp.int32)
    q_doc = jnp.zeros((1, KEYS), jnp.int32)
    for s in range(GRP):
        block = order[GRP * g + s]
        q_pos = jnp.where(slot_of == s, block * BLK + in_slot, q_pos)
        q_doc = jnp.where(slot_of == s, doc[block], q_doc)

    m_ref[...] = jnp.full(m_ref.shape, NEG, F32)
    mass_ref[...] = jnp.zeros(mass_ref.shape, F32)
    ws_ref[...] = jnp.zeros(ws_ref.shape, F32)

    def latents_of(d):
        return jnp.concatenate(
            [
                jnp.concatenate([lat_buf[d, s, c * BLK : (c + 1) * BLK] for c in range(COLS)], axis=1)
                for s in range(GRP)
            ],
            axis=0,
        )

    def half_rows(rows, half):
        return jnp.concatenate(
            [rows[s * BLK + half * HALF : s * BLK + half * HALF + HALF] for s in range(GRP)], axis=0
        )

    def scores_tile(d, local):
        kv = nn(latents_of(d), w_head[...]).astype(BF16)
        rope = jnp.concatenate([lat_buf[d, s, LAT:] for s in range(GRP)], axis=0)
        top = jnp.full((8, KEYS), NEG, F32)
        for half in range(2):
            k_buf[d, half] = jnp.concatenate([half_rows(kv[:, :NOPE], half), rope], axis=1)
            scores = nt(k_buf[d, half], (q_lo, q_hi)[half][...])
            for s in range(GRP):
                block = order[GRP * (g - d) + s]
                same = q_doc == doc[block]
                part = scores[s * HALF : s * HALF + HALF] * (SCALE * LOG2E)
                if local:
                    pos = lax.broadcasted_iota(jnp.int32, (HALF, 1), 0) + (block * BLK + half * HALF)
                    part = jnp.where(same & (pos <= q_pos), part, NEG)
                else:
                    part = part + jnp.where(same, 0.0, NEG)
                p_buf[d, half, s] = part
                top = jnp.maximum(top, jnp.max(part.reshape(HALF // 8, 8, KEYS), axis=0))
        peak = jnp.max(top, axis=0, keepdims=True)
        mass = jnp.zeros((8, KEYS), F32)
        weighted = jnp.zeros((8, KEYS), F32)
        for half in range(2):
            dp = nt(half_rows(kv[:, NOPE:], half), g_out[...])
            for s in range(GRP):
                here = dp[s * HALF : s * HALF + HALF]
                p = jnp.exp2(p_buf[d, half, s] - peak)
                p_buf[d, half, s] = p
                dp_buf[d, half, s] = here
                mass = mass + jnp.sum(p.reshape(HALF // 8, 8, KEYS), axis=0)
                weighted = weighted + jnp.sum((p * here).reshape(HALF // 8, 8, KEYS), axis=0)
        m_ref[d] = peak
        mass_ref[d] = jnp.sum(mass, axis=0, keepdims=True)
        ws_ref[d] = jnp.sum(weighted, axis=0, keepdims=True)

    def spread(d):
        @pl.when((d <= window) & (g >= d) & (d % SIDE != 0))
        def _():
            arrived(lat_buf.at[d, j], r_far.at[d], beside)
            near_copy(d).start()
            own_copy(d).start()

    def hand_on(d):
        @pl.when((d >= 0) & (d <= window) & (g >= d))
        def _():
            arrived(lat_buf.at[d, j_near], r_near.at[d], beside)
            pass_copy(d).start()

    def whole(d):
        arrived(lat_buf.at[d, j_core], r_own.at[d], beside)
        arrived(lat_buf.at[d, j_next], r_pass.at[d], beside)

    hand_on(0)

    @pl.when(y >= 1)
    def _():
        arrived(lat_buf.at[SIDE, j], r_far.at[SIDE], beside)

        @pl.when(y + 1 < SIDE)
        def _():
            down_copy(1).start()

        near_copy(SIDE).start()
        own_copy(SIDE).start()

    fan(1)
    for i in range(1, GRP):
        arrived(q_buf.at[(j + GRP - i) % GRP], r_q.at[i], mate(i))
    blank = jnp.zeros((HALF, ROPE), BF16)
    for s in range(GRP):
        at = s * BLK
        pair = q_buf[s, 2 * BLK :]
        first, second = pair[:, :ROPE], pair[:, ROPE:]
        q_lo[at : at + BLK, :NOPE] = q_buf[s, :BLK]
        q_hi[at : at + BLK, :NOPE] = q_buf[s, :BLK]
        g_out[at : at + BLK] = q_buf[s, BLK : 2 * BLK]
        q_lo[at : at + HALF, NOPE:] = jnp.concatenate([first, blank], axis=1)
        q_lo[at + HALF : at + BLK, NOPE:] = jnp.concatenate([second, blank], axis=1)
        q_hi[at : at + HALF, NOPE:] = jnp.concatenate([blank, first], axis=1)
        q_hi[at + HALF : at + BLK, NOPE:] = jnp.concatenate([blank, second], axis=1)
    whole(0)
    weights.wait()
    scores_tile(0, True)

    @pl.when(y >= 2)
    def _():
        arrived(lat_buf.at[2 * SIDE, j], r_far.at[2 * SIDE], beside)
        near_copy(2 * SIDE).start()
        own_copy(2 * SIDE).start()

    fan(2)

    def far_scores(i, carry):
        spread(i)

        @pl.when(i > PASS_LAG)
        def _():
            hand_on(i - PASS_LAG)

        @pl.when((i > TILE_LAG) & (g >= i - TILE_LAG))
        def _():
            whole(i - TILE_LAG)
            scores_tile(i - TILE_LAG, False)

        return carry

    lax.fori_loop(1, window + TILE_LAG + 1, far_scores, 0)

    peak = jnp.max(m_ref[...], axis=0)
    factors = jnp.exp2(m_ref[...] - peak[None])
    mass = jnp.sum(mass_ref[...] * factors, axis=0)
    weighted = jnp.sum(ws_ref[...] * factors, axis=0)
    fac_ref[...] = factors / mass[None]
    delta_ref[...] = weighted / mass
    dqn[...] = jnp.zeros(dqn.shape, F32)
    dqr[...] = jnp.zeros(dqr.shape, F32)
    dw_acc[...] = jnp.zeros(dw_acc.shape, F32)

    def grads_tile(d):
        factor = fac_ref[d]
        delta = delta_ref[...]
        rope_sum = None
        pairs = []
        for half in range(2):
            mixed, probs = [], []
            for s in range(GRP):
                p = p_buf[d, half, s] * factor
                mixed.append((p * (dp_buf[d, half, s] - delta)).astype(BF16))
                probs.append(p.astype(BF16))
            mixed = jnp.concatenate(mixed, axis=0)
            probs = jnp.concatenate(probs, axis=0)
            d_keys = nn(mixed, (q_lo, q_hi)[half][...]) * SCALE
            d_values = nn(probs, g_out[...])
            rope_sum = d_keys[:, NOPE:] if half == 0 else rope_sum + d_keys[:, NOPE:]
            pairs.append(jnp.concatenate([d_keys[:, :NOPE], d_values], axis=1).astype(BF16))
            dq = tn(k_buf[d, half], mixed)
            dqn[...] += dq[:NOPE]
            dqr[...] += dq[NOPE + half * ROPE : NOPE + half * ROPE + ROPE]
        pairs = jnp.concatenate(
            [pairs[half][s * HALF : s * HALF + HALF] for s in range(GRP) for half in range(2)], axis=0
        )
        d_lat = nt(pairs, w_head[...])
        for s in range(GRP):
            for c in range(COLS):
                part = d_lat[s * BLK : (s + 1) * BLK, c * BLK : (c + 1) * BLK]
                terms[d, s, c * BLK : (c + 1) * BLK] = part.astype(BF16)
            terms[d, s, LAT:] = rope_sum[s * HALF : s * HALF + HALF].astype(BF16)
        dw_acc[...] += tn(pairs, latents_of(d))

    def tc_copy(d):
        return remote(terms.at[d, j_core], core_recv.at[d, 0], s_tc.at[d], r_tc.at[d], beside)

    def tx_copy(d):
        return remote(terms.at[d, j_next], core_recv.at[d, 1], s_tx.at[d], r_tx.at[d], beside)

    def tn_copy(d):
        return remote(near_send.at[d], near_recv.at[d], s_tn.at[d], r_tn.at[d], behind)

    def tf_copy(d):
        return remote(far_send.at[d], far_recv.at[d], s_tf.at[d], r_tf.at[d], row_mate(4 * SIDE - d))

    def tf_corner():
        d = window
        return remote(far_send.at[d], far_recv.at[d], s_tf.at[d], r_tf.at[d], other(groups - d))

    def up_copy(dy):
        to = ((g - SIDE) * GRP + j, hz)
        return remote(up_send.at[dy], up_recv.at[dy], s_up.at[dy], r_up.at[dy], to)

    def chip_sum(d):
        @pl.when((d <= window) & (g >= d))
        def _():
            arrived(core_recv.at[d, 1], r_tx.at[d], beside)
            near_send[d] = (terms[d, j_near].astype(F32) + core_recv[d, 1].astype(F32)).astype(BF16)
            tn_copy(d).start()

    def slot_sum(d):
        arrived(core_recv.at[d, 0], r_tc.at[d], beside)
        arrived(near_recv.at[d], r_tn.at[d], beside)
        return terms[d, j].astype(F32) + core_recv[d, 0].astype(F32) + near_recv[d].astype(F32)

    def send_terms(d):
        @pl.when((d <= window) & (g >= d))
        def _():
            far_send[d] = slot_sum(d).astype(BF16)

            @pl.when((d % SIDE != 0) & ((d < window) | (x > 0)))
            def _():
                tf_copy(d).start()

            @pl.when((d == window) & (x == 0))
            def _():
                tf_corner().start()

    def far_grads(step, carry):
        d = window - step

        @pl.when(g >= d)
        def _():
            grads_tile(d)
            tx_copy(d).start()
            tc_copy(d).start()

        chip_sum(d + CHIP_LAG)
        send_terms(d + SLOT_LAG)
        return carry

    lax.fori_loop(0, window + 1, far_grads, 0)
    for d in range(CHIP_LAG - 1, -1, -1):
        chip_sum(d)

    dq_nope = (dqn[...] * SCALE).T.astype(BF16)
    dq_rope = (dqr[...] * SCALE).T.astype(BF16)
    for s in range(GRP):
        dq_send[s, :BLK] = dq_nope[s * BLK : s * BLK + BLK]
        dq_send[s, BLK:] = pack_halves(dq_rope[s * BLK : s * BLK + BLK])
    dq_recv[j] = dq_send[j]

    def dq_copy(i):
        return remote(dq_send.at[(j + i) % GRP], dq_recv.at[j], s_dq.at[i], r_dq.at[i], mate(i))

    for i in range(1, GRP):
        dq_copy(i).start()

    def add(ref, sem):
        arrived(ref, sem, beside)
        total[...] += ref[...].astype(F32)

    def row_sum(dy):
        for i in (1, 3, 2):
            d = SIDE * dy + (x + i) % SIDE - x

            @pl.when((d >= 1) & (d <= window))
            def _():
                add(far_recv.at[d], r_tf.at[d])

    for d in range(SLOT_LAG - 1, 3, -1):
        send_terms(d)

    @pl.when(y >= 2)
    def _():
        total[...] = far_send[2 * SIDE].astype(F32)
        row_sum(2)
        up_send[1] = total[...].astype(BF16)
        up_copy(1).start()

    for d in range(min(SLOT_LAG - 1, 3), 0, -1):
        send_terms(d)

    @pl.when(y >= 1)
    def _():
        total[...] = far_send[SIDE].astype(F32)
        row_sum(1)

        @pl.when(y + 1 < SIDE)
        def _():
            add(up_recv.at[1], r_up.at[1])

        up_send[0] = total[...].astype(BF16)
        up_copy(0).start()

    grad_w = dw_acc[...].T.astype(BF16)
    for i in range(groups):
        dw_send[i] = grad_w[i * w_rows : (i + 1) * w_rows]

    def dw_copy(i):
        return remote(dw_send.at[(g + i) % groups], dw_recv.at[i], s_dw.at[i], r_dw.at[i], other(i))

    def send_dw(i, carry):
        dw_copy(i).start()
        return carry

    lax.fori_loop(1, groups, send_dw, 0)

    total[...] = slot_sum(0)
    row_sum(0)

    @pl.when(corner_out)
    def _():
        add(far_recv.at[window], r_tf.at[window])

    @pl.when(y + 1 < SIDE)
    def _():
        add(up_recv.at[0], r_up.at[0])

    for t in range(zs):
        for c in range(COLS):
            z_send[t, c * z_rows : (c + 1) * z_rows] = total[
                c * BLK + t * z_rows : c * BLK + (t + 1) * z_rows
            ].astype(BF16)
        z_send[t, COLS * z_rows :] = total[LAT + t * zp_rows : LAT + (t + 1) * zp_rows].astype(BF16)

    def z_copy(i):
        return remote(z_send.at[(hz + i) % zs], z_recv.at[i], s_z.at[i], r_z.at[i], deep(i))

    for i in range(1, zs):
        z_copy(i).start()

    for i in range(1, GRP):
        arrived(dq_recv.at[(j + GRP - i) % GRP], r_dq.at[i], mate(i))
    columns = []
    for h in range(GRP):
        columns += [dq_recv[h, :BLK], unpack_halves(dq_recv[h, BLK:])]
    dq_out[...] = jnp.concatenate(columns, axis=1)

    z_sum = z_send[hz].astype(F32)
    for i in range(1, zs):
        arrived(z_recv.at[i], r_z.at[i], deep(i))
        z_sum = z_sum + z_recv[i].astype(F32)
    z_fin[hz] = z_sum.astype(BF16)

    def zf_copy(i):
        return remote(z_fin.at[hz], z_fin.at[hz], s_zf.at[i], r_zf.at[i], deep(i))

    for i in range(1, zs):
        zf_copy(i).start()

    dw_sum[...] = dw_send[g].astype(F32)

    def take_dw(i, carry):
        arrived(dw_recv.at[i], r_dw.at[i], other(i))
        dw_sum[...] += dw_recv[i].astype(F32)
        return carry

    lax.fori_loop(1, groups, take_dw, 0)

    def dwf_copy(i):
        rows = pl.ds(pl.multiple_of((j + i) % GRP * o_rows, o_rows), o_rows)
        return remote(dw_sum.at[rows], dw_fin.at[j], s_dwf.at[i], r_dwf.at[i], mate(i))

    for i in range(1, GRP):
        dwf_copy(i).start()
    dw_fin[j] = dw_sum[pl.ds(pl.multiple_of(j * o_rows, o_rows), o_rows)]

    for i in range(1, zs):
        arrived(z_fin.at[(hz + zs - i) % zs], r_zf.at[i], deep(i))
    packed = []
    for t in range(zs):
        for c in range(COLS):
            part = z_fin[t, c * z_rows : (c + 1) * z_rows].astype(F32)
            dlat_out[t * z_rows : (t + 1) * z_rows, c * BLK : (c + 1) * BLK] = part
        packed.append(z_fin[t, COLS * z_rows :].astype(F32))
    packed = jnp.concatenate(packed, axis=0).T
    drope_out[...] = jnp.concatenate([packed[:ROPE], packed[ROPE:]], axis=1)

    for i in range(1, GRP):
        arrived(dw_fin.at[(j + GRP - i) % GRP], r_dwf.at[i], mate(i))
    dw_out[...] = jnp.concatenate([dw_fin[h] for h in range(GRP)], axis=1)

    for i in range(1, GRP):
        q_copy(i).wait_send()
        dq_copy(i).wait_send()
        dwf_copy(i).wait_send()
    for i in range(1, zs):
        z_copy(i).wait_send()
        zf_copy(i).wait_send()

    def end_blocks(d, carry):
        @pl.when(g >= d)
        def _():
            own_copy(d).wait_send()
            near_copy(d).wait_send()
            pass_copy(d).wait_send()
            tc_copy(d).wait_send()
            tx_copy(d).wait_send()
            tn_copy(d).wait_send()

        @pl.when((d % SIDE != 0) & (g >= d))
        def _():
            tf_copy(d).wait_send()

        return carry

    lax.fori_loop(0, window + 1, end_blocks, 0)
    for dy in range(2):

        @pl.when((y + 1 < SIDE) & (y >= dy))
        def _():
            down_copy(dy).wait_send()

        @pl.when(y > dy)
        def _():
            up_copy(dy).wait_send()

    for dy in range(3):
        for i in (1, 3, 2):

            @pl.when(in_fan(dy, i))
            def _():
                fan_copy(dy, i).wait_send()

    @pl.when(corner_out)
    def _():
        corner_copy().wait_send()


    def end_dw(i, carry):
        dw_copy(i).wait_send()
        return carry

    lax.fori_loop(1, groups, end_dw, 0)


def solution(mesh):
    groups = mesh.shape["ctx"] // GRP
    zs = mesh.shape["head"]
    span = min(groups - 1, (MOST + GRP - 2) // GRP) + 1
    w_rows = LAT // groups
    z_piece = PIECE // zs
    vmem = pltpu.VMEM
    dma = pltpu.SemaphoreType.DMA
    scratch = [
        vmem((GRP, ROWS, 128), BF16),
        vmem((GRP, ROWS, 128), BF16),
        vmem((span, GRP, PIECE, 128), BF16),
        vmem((span, 2, KEYS // 2, 256), BF16),
        vmem((LAT, 256), BF16),
        vmem((KEYS, 256), BF16),
        vmem((KEYS, 256), BF16),
        vmem((KEYS, VDIM), BF16),
        vmem((span, 2, GRP, HALF, KEYS), F32),
        vmem((span, 2, GRP, HALF, KEYS), F32),
        vmem((span, 1, KEYS), F32),
        vmem((span, 1, KEYS), F32),
        vmem((span, 1, KEYS), F32),
        vmem((span, 1, KEYS), F32),
        vmem((1, KEYS), F32),
        vmem((NOPE, KEYS), F32),
        vmem((ROPE, KEYS), F32),
        vmem((256, LAT), F32),
        vmem((span, GRP, PIECE, 128), BF16),
        vmem((span, 2, PIECE, 128), BF16),
        vmem((span, PIECE, 128), BF16),
        vmem((span, PIECE, 128), BF16),
        vmem((span, PIECE, 128), BF16),
        vmem((span, PIECE, 128), BF16),
        vmem((2, PIECE, 128), BF16),
        vmem((2, PIECE, 128), BF16),
        vmem((PIECE, 128), F32),
        vmem((groups, w_rows, 256), BF16),
        vmem((groups, w_rows, 256), BF16),
        vmem((w_rows, 256), F32),
        vmem((GRP, w_rows // GRP, 256), F32),
        vmem((GRP, BLK + HALF, 128), BF16),
        vmem((GRP, BLK + HALF, 128), BF16),
        vmem((zs, z_piece, 128), BF16),
        vmem((zs, z_piece, 128), BF16),
        vmem((zs, z_piece, 128), BF16),
    ]
    scratch += [dma((1,)), dma((GRP,)), dma((GRP,)), dma((2,)), dma((3, SIDE)), dma((1,)), dma((span,))]
    for count in (*[span] * 7, 2, groups, GRP, GRP, zs, zs):
        scratch += [dma((count,)), dma((count,))]

    def local(query, latent, k_rope, d_out, w_kv, block_doc, block_order):
        whole = pl.BlockSpec(memory_space=pltpu.VMEM)
        scalars = pl.BlockSpec(memory_space=pltpu.SMEM)
        anywhere = pl.BlockSpec(memory_space=pl.ANY)
        results = pl.pallas_call(
            functools.partial(kernel, groups, zs),
            out_shape=(
                jax.ShapeDtypeStruct(query.shape, BF16),
                jax.ShapeDtypeStruct((BLK, LAT), F32),
                jax.ShapeDtypeStruct((ROPE, BLK), F32),
                jax.ShapeDtypeStruct((w_rows // GRP, GRP * 256), F32),
            ),
            in_specs=[whole] * 4 + [anywhere] + [scalars] * 2,
            out_specs=(whole,) * 4,
            scratch_shapes=scratch,
            compiler_params=pltpu.CompilerParams(
                collective_id=0, has_side_effects=True, vmem_limit_bytes=56 * 1024 * 1024
            ),
        )(query, latent, k_rope.T, d_out, w_kv, block_doc, block_order)
        d_query, d_latent, d_rope, d_w_kv = pl.pallas_call(
            keep,
            out_shape=tuple(jax.ShapeDtypeStruct(r.shape, r.dtype) for r in results),
            in_specs=[whole] * 4,
            out_specs=(whole,) * 4,
        )(*results)
        return d_query, d_latent, d_rope.T, d_w_kv

    return jax.shard_map(
        local,
        mesh=mesh,
        in_specs=(
            P("ctx", "head"),
            P("ctx", None),
            P("ctx", None),
            P("ctx", "head"),
            P(None, "head"),
            P(),
            P(),
        ),
        out_specs=(P("ctx", "head"), P("ctx", None), P("ctx", None), P("ctx", "head")),
        check_vma=False,
    )
```

```python
import functools
import math

import jax
import jax.numpy as jnp
from jax import lax
from jax.experimental import pallas as pl
from jax.experimental.pallas import tpu as pltpu
from jax.sharding import PartitionSpec as P

LAT = 512
ROPE = 64
NOPE = 128
VDIM = 128
BLK = 128
HEAD = NOPE + ROPE
HALF = BLK // 2
SIDE = 4
GRP = 4
KEYS = GRP * BLK
ROWS = 2 * BLK + HALF
COLS = LAT // BLK
PIECE = LAT + HALF
PASS_LAG, TILE_LAG = 3, 5
CHIP_LAG, SLOT_LAG = 2, 5
MOST = 36
SCALE = HEAD**-0.5
LOG2E = math.log2(math.e)
NEG = -1e30
MESH = pl.DeviceIdType.MESH
F32 = jnp.float32
BF16 = jnp.bfloat16


def nt(a, b):
    return lax.dot_general(a, b, (((1,), (1,)), ((), ())), preferred_element_type=F32)


def tn(a, b):
    return lax.dot_general(a, b, (((0,), (0,)), ((), ())), preferred_element_type=F32)


def nn(a, b):
    return jnp.dot(a, b, preferred_element_type=F32)


def pack_halves(rows):
    return jnp.concatenate([rows[:HALF], rows[HALF:]], axis=1)


def unpack_halves(rows):
    return jnp.concatenate([rows[:, :ROPE], rows[:, ROPE:]], axis=0)


def keep(a, b, c, d, a_out, b_out, c_out, d_out):
    for src, dst in ((a, a_out), (b, b_out), (c, c_out), (d, d_out)):
        dst[...] = src[...]


def kernel(
    groups,
    zs,
    query,
    latent,
    k_rope,
    d_out,
    w_kv,
    doc,
    order,
    dq_out,
    dlat_out,
    drope_out,
    dw_out,
    q_stage,
    q_buf,
    lat_buf,
    k_buf,
    w_head,
    q_lo,
    q_hi,
    g_out,
    p_buf,
    dp_buf,
    m_ref,
    mass_ref,
    ws_ref,
    fac_ref,
    delta_ref,
    dqn,
    dqr,
    dw_acc,
    terms,
    core_recv,
    near_send,
    near_recv,
    far_send,
    far_recv,
    up_send,
    up_recv,
    total,
    dw_send,
    dw_recv,
    dw_sum,
    dw_fin,
    dq_send,
    dq_recv,
    z_send,
    z_recv,
    z_fin,
    s_w,
    s_q,
    r_q,
    s_down,
    s_fan,
    s_corner,
    r_far,
    s_own,
    r_own,
    s_near,
    r_near,
    s_pass,
    r_pass,
    s_tc,
    r_tc,
    s_tx,
    r_tx,
    s_tn,
    r_tn,
    s_tf,
    r_tf,
    s_up,
    r_up,
    s_dw,
    r_dw,
    s_dwf,
    r_dwf,
    s_dq,
    r_dq,
    s_z,
    r_z,
    s_zf,
    r_zf,
):
    ctx = lax.axis_index("ctx")
    hz = lax.axis_index("head")
    g = ctx // GRP
    j = ctx % GRP
    z_lo = j // 2
    core = j % 2
    j_core = 2 * z_lo + 1 - core
    j_near = 2 * (1 - z_lo) + core
    j_next = 2 * (1 - z_lo) + 1 - core
    window = min(groups - 1, (MOST + GRP - 2) // GRP)
    y = g // SIDE
    x = g % SIDE
    w_rows = LAT // groups
    o_rows = w_rows // GRP
    z_rows = BLK // zs
    zp_rows = HALF // zs

    def mate(i):
        return ((g * GRP + (j + i) % GRP), hz)

    def other(i):
        return (((g + i) % groups) * GRP + j, hz)

    def deep(i):
        return (ctx, (hz + i) % zs)

    beside = (g * GRP + j_core, hz)
    ahead = (g * GRP + j_near, (hz + z_lo + core * (zs - 1)) % zs)
    behind = (g * GRP + j_near, (hz + z_lo + (1 - core) * (zs - 1)) % zs)

    def remote(src, dst, send, recv, to):
        return pltpu.make_async_remote_copy(
            src_ref=src, dst_ref=dst, send_sem=send, recv_sem=recv, device_id=to, device_id_type=MESH
        )

    def arrived(ref, sem, to):
        remote(ref, ref, sem, sem, to).wait_recv()

    columns = pl.ds(pl.multiple_of(j * 256, 256), 256)
    weights = pltpu.make_async_copy(w_kv.at[:, columns], w_head, s_w.at[0])
    weights.start()
    barrier = pltpu.get_barrier_semaphore()
    for i in range(1, GRP):
        pl.semaphore_signal(barrier, inc=1, device_id=mate(i), device_id_type=MESH)
    for i in range(1, zs):
        pl.semaphore_signal(barrier, inc=1, device_id=deep(i), device_id_type=MESH)
    pl.semaphore_signal(barrier, inc=1, device_id=ahead, device_id_type=MESH)
    pl.semaphore_signal(barrier, inc=1, device_id=behind, device_id_type=MESH)

    def greet(i, carry):
        pl.semaphore_signal(barrier, inc=1, device_id=other(i), device_id_type=MESH)
        return carry

    lax.fori_loop(1, groups, greet, 0)

    for c in range(COLS):
        lat_buf[0, j, c * BLK : (c + 1) * BLK] = latent[:, c * BLK : (c + 1) * BLK]
    lat_buf[0, j, LAT:] = pack_halves(k_rope[...].astype(F32).T.astype(BF16))
    for h in range(GRP):
        q_stage[h, :BLK] = query[:, HEAD * h : HEAD * h + NOPE]
        q_stage[h, BLK : 2 * BLK] = d_out[:, VDIM * h : VDIM * h + VDIM]
        q_stage[h, 2 * BLK :] = pack_halves(query[:, HEAD * h + NOPE : HEAD * h + HEAD])

    pl.semaphore_wait(barrier, GRP - 1 + zs - 1 + 2 + groups - 1)

    def row_mate(i):
        return ((g - x + (x + i) % SIDE) * GRP + j, hz)

    def down_copy(dy):
        here, there = SIDE * dy, SIDE * (dy + 1)
        to = ((g + SIDE) * GRP + j, hz)
        return remote(lat_buf.at[here, j], lat_buf.at[there, j], s_down.at[dy], r_far.at[there], to)

    def fan_copy(dy, i):
        d = SIDE * dy + (x + i) % SIDE - x
        return remote(lat_buf.at[SIDE * dy, j], lat_buf.at[d, j], s_fan.at[dy, i], r_far.at[d], row_mate(i))

    def in_fan(dy, i):
        d = SIDE * dy + (x + i) % SIDE - x
        return (y >= dy) & (d >= 1) & (d <= window)

    corner_out = (y == 0) & (x == SIDE - 1)

    def corner_copy():
        return remote(lat_buf.at[0, j], lat_buf.at[window, j], s_corner.at[0], r_far.at[window], other(window))

    def fan(dy):
        for i in (1, 3, 2):

            @pl.when(in_fan(dy, i))
            def _():
                fan_copy(dy, i).start()

    def own_copy(d):
        return remote(lat_buf.at[d, j], lat_buf.at[d, j], s_own.at[d], r_own.at[d], beside)

    def near_copy(d):
        return remote(lat_buf.at[d, j], lat_buf.at[d, j], s_near.at[d], r_near.at[d], ahead)

    def pass_copy(d):
        return remote(lat_buf.at[d, j_near], lat_buf.at[d, j_near], s_pass.at[d], r_pass.at[d], beside)

    def q_copy(i):
        return remote(q_stage.at[(j + i) % GRP], q_buf.at[j], s_q.at[i], r_q.at[i], mate(i))

    near_copy(0).start()
    own_copy(0).start()

    @pl.when(y + 1 < SIDE)
    def _():
        down_copy(0).start()

    fan(0)

    @pl.when(corner_out)
    def _():
        corner_copy().start()

    for i in range(1, GRP):
        q_copy(i).start()
    q_buf[j] = q_stage[j]

    slot_of = lax.broadcasted_iota(jnp.int32, (1, KEYS), 1) // BLK
    in_slot = lax.broadcasted_iota(jnp.int32, (1, KEYS), 1) % BLK
    q_pos = jnp.zeros((1, KEYS), jnp.int32)
    q_doc = jnp.zeros((1, KEYS), jnp.int32)
    for s in range(GRP):
        block = order[GRP * g + s]
        q_pos = jnp.where(slot_of == s, block * BLK + in_slot, q_pos)
        q_doc = jnp.where(slot_of == s, doc[block], q_doc)

    m_ref[...] = jnp.full(m_ref.shape, NEG, F32)
    mass_ref[...] = jnp.zeros(mass_ref.shape, F32)
    ws_ref[...] = jnp.zeros(ws_ref.shape, F32)

    def latents_of(d):
        return jnp.concatenate(
            [
                jnp.concatenate([lat_buf[d, s, c * BLK : (c + 1) * BLK] for c in range(COLS)], axis=1)
                for s in range(GRP)
            ],
            axis=0,
        )

    def half_rows(rows, half):
        return jnp.concatenate(
            [rows[s * BLK + half * HALF : s * BLK + half * HALF + HALF] for s in range(GRP)], axis=0
        )

    def scores_tile(d, local):
        kv = nn(latents_of(d), w_head[...]).astype(BF16)
        rope = jnp.concatenate([lat_buf[d, s, LAT:] for s in range(GRP)], axis=0)
        top = jnp.full((8, KEYS), NEG, F32)
        for half in range(2):
            k_buf[d, half] = jnp.concatenate([half_rows(kv[:, :NOPE], half), rope], axis=1)
            scores = nt(k_buf[d, half], (q_lo, q_hi)[half][...])
            for s in range(GRP):
                block = order[GRP * (g - d) + s]
                same = q_doc == doc[block]
                part = scores[s * HALF : s * HALF + HALF] * (SCALE * LOG2E)
                if local:
                    pos = lax.broadcasted_iota(jnp.int32, (HALF, 1), 0) + (block * BLK + half * HALF)
                    part = jnp.where(same & (pos <= q_pos), part, NEG)
                else:
                    part = part + jnp.where(same, 0.0, NEG)
                p_buf[d, half, s] = part
                top = jnp.maximum(top, jnp.max(part.reshape(HALF // 8, 8, KEYS), axis=0))
        peak = jnp.max(top, axis=0, keepdims=True)
        mass = jnp.zeros((8, KEYS), F32)
        weighted = jnp.zeros((8, KEYS), F32)
        for half in range(2):
            dp = nt(half_rows(kv[:, NOPE:], half), g_out[...])
            for s in range(GRP):
                here = dp[s * HALF : s * HALF + HALF]
                p = jnp.exp2(p_buf[d, half, s] - peak)
                p_buf[d, half, s] = p
                dp_buf[d, half, s] = here
                mass = mass + jnp.sum(p.reshape(HALF // 8, 8, KEYS), axis=0)
                weighted = weighted + jnp.sum((p * here).reshape(HALF // 8, 8, KEYS), axis=0)
        m_ref[d] = peak
        mass_ref[d] = jnp.sum(mass, axis=0, keepdims=True)
        ws_ref[d] = jnp.sum(weighted, axis=0, keepdims=True)

    def spread(d):
        @pl.when((d <= window) & (g >= d) & (d % SIDE != 0))
        def _():
            arrived(lat_buf.at[d, j], r_far.at[d], beside)
            near_copy(d).start()
            own_copy(d).start()

    def hand_on(d):
        @pl.when((d >= 0) & (d <= window) & (g >= d))
        def _():
            arrived(lat_buf.at[d, j_near], r_near.at[d], beside)
            pass_copy(d).start()

    def whole(d):
        arrived(lat_buf.at[d, j_core], r_own.at[d], beside)
        arrived(lat_buf.at[d, j_next], r_pass.at[d], beside)

    hand_on(0)

    @pl.when(y >= 1)
    def _():
        arrived(lat_buf.at[SIDE, j], r_far.at[SIDE], beside)

        @pl.when(y + 1 < SIDE)
        def _():
            down_copy(1).start()

        near_copy(SIDE).start()
        own_copy(SIDE).start()

    fan(1)
    for i in range(1, GRP):
        arrived(q_buf.at[(j + GRP - i) % GRP], r_q.at[i], mate(i))
    blank = jnp.zeros((HALF, ROPE), BF16)
    for s in range(GRP):
        at = s * BLK
        pair = q_buf[s, 2 * BLK :]
        first, second = pair[:, :ROPE], pair[:, ROPE:]
        q_lo[at : at + BLK, :NOPE] = q_buf[s, :BLK]
        q_hi[at : at + BLK, :NOPE] = q_buf[s, :BLK]
        g_out[at : at + BLK] = q_buf[s, BLK : 2 * BLK]
        q_lo[at : at + HALF, NOPE:] = jnp.concatenate([first, blank], axis=1)
        q_lo[at + HALF : at + BLK, NOPE:] = jnp.concatenate([second, blank], axis=1)
        q_hi[at : at + HALF, NOPE:] = jnp.concatenate([blank, first], axis=1)
        q_hi[at + HALF : at + BLK, NOPE:] = jnp.concatenate([blank, second], axis=1)
    whole(0)
    weights.wait()
    scores_tile(0, True)

    @pl.when(y >= 2)
    def _():
        arrived(lat_buf.at[2 * SIDE, j], r_far.at[2 * SIDE], beside)
        near_copy(2 * SIDE).start()
        own_copy(2 * SIDE).start()

    fan(2)

    def far_scores(i, carry):
        spread(i)

        @pl.when(i > PASS_LAG)
        def _():
            hand_on(i - PASS_LAG)

        @pl.when((i > TILE_LAG) & (g >= i - TILE_LAG))
        def _():
            whole(i - TILE_LAG)
            scores_tile(i - TILE_LAG, False)

        return carry

    lax.fori_loop(1, window + TILE_LAG + 1, far_scores, 0)

    peak = jnp.max(m_ref[...], axis=0)
    factors = jnp.exp2(m_ref[...] - peak[None])
    mass = jnp.sum(mass_ref[...] * factors, axis=0)
    weighted = jnp.sum(ws_ref[...] * factors, axis=0)
    fac_ref[...] = factors / mass[None]
    delta_ref[...] = weighted / mass
    dqn[...] = jnp.zeros(dqn.shape, F32)
    dqr[...] = jnp.zeros(dqr.shape, F32)
    dw_acc[...] = jnp.zeros(dw_acc.shape, F32)

    def grads_tile(d):
        factor = fac_ref[d]
        delta = delta_ref[...]
        rope_sum = None
        pairs = []
        for half in range(2):
            mixed, probs = [], []
            for s in range(GRP):
                p = p_buf[d, half, s] * factor
                mixed.append((p * (dp_buf[d, half, s] - delta)).astype(BF16))
                probs.append(p.astype(BF16))
            mixed = jnp.concatenate(mixed, axis=0)
            probs = jnp.concatenate(probs, axis=0)
            d_keys = nn(mixed, (q_lo, q_hi)[half][...]) * SCALE
            d_values = nn(probs, g_out[...])
            rope_sum = d_keys[:, NOPE:] if half == 0 else rope_sum + d_keys[:, NOPE:]
            pairs.append(jnp.concatenate([d_keys[:, :NOPE], d_values], axis=1).astype(BF16))
            dq = tn(k_buf[d, half], mixed)
            dqn[...] += dq[:NOPE]
            dqr[...] += dq[NOPE + half * ROPE : NOPE + half * ROPE + ROPE]
        pairs = jnp.concatenate(
            [pairs[half][s * HALF : s * HALF + HALF] for s in range(GRP) for half in range(2)], axis=0
        )
        d_lat = nt(pairs, w_head[...])
        for s in range(GRP):
            for c in range(COLS):
                part = d_lat[s * BLK : (s + 1) * BLK, c * BLK : (c + 1) * BLK]
                terms[d, s, c * BLK : (c + 1) * BLK] = part.astype(BF16)
            terms[d, s, LAT:] = rope_sum[s * HALF : s * HALF + HALF].astype(BF16)
        dw_acc[...] += tn(pairs, latents_of(d))

    def tc_copy(d):
        return remote(terms.at[d, j_core], core_recv.at[d, 0], s_tc.at[d], r_tc.at[d], beside)

    def tx_copy(d):
        return remote(terms.at[d, j_next], core_recv.at[d, 1], s_tx.at[d], r_tx.at[d], beside)

    def tn_copy(d):
        return remote(near_send.at[d], near_recv.at[d], s_tn.at[d], r_tn.at[d], behind)

    def tf_copy(d):
        return remote(far_send.at[d], far_recv.at[d], s_tf.at[d], r_tf.at[d], row_mate(4 * SIDE - d))

    def tf_corner():
        d = window
        return remote(far_send.at[d], far_recv.at[d], s_tf.at[d], r_tf.at[d], other(groups - d))

    def up_copy(dy):
        to = ((g - SIDE) * GRP + j, hz)
        return remote(up_send.at[dy], up_recv.at[dy], s_up.at[dy], r_up.at[dy], to)

    def chip_sum(d):
        @pl.when((d <= window) & (g >= d))
        def _():
            arrived(core_recv.at[d, 1], r_tx.at[d], beside)
            near_send[d] = (terms[d, j_near].astype(F32) + core_recv[d, 1].astype(F32)).astype(BF16)
            tn_copy(d).start()

    def slot_sum(d):
        arrived(core_recv.at[d, 0], r_tc.at[d], beside)
        arrived(near_recv.at[d], r_tn.at[d], beside)
        return terms[d, j].astype(F32) + core_recv[d, 0].astype(F32) + near_recv[d].astype(F32)

    def send_terms(d):
        @pl.when((d <= window) & (g >= d))
        def _():
            far_send[d] = slot_sum(d).astype(BF16)

            @pl.when((d % SIDE != 0) & ((d < window) | (x > 0)))
            def _():
                tf_copy(d).start()

            @pl.when((d == window) & (x == 0))
            def _():
                tf_corner().start()

    def far_grads(step, carry):
        d = window - step

        @pl.when(g >= d)
        def _():
            grads_tile(d)
            tx_copy(d).start()
            tc_copy(d).start()

        chip_sum(d + CHIP_LAG)
        send_terms(d + SLOT_LAG)
        return carry

    lax.fori_loop(0, window + 1, far_grads, 0)
    for d in range(CHIP_LAG - 1, -1, -1):
        chip_sum(d)

    dq_nope = (dqn[...] * SCALE).T.astype(BF16)
    dq_rope = (dqr[...] * SCALE).T.astype(BF16)
    for s in range(GRP):
        dq_send[s, :BLK] = dq_nope[s * BLK : s * BLK + BLK]
        dq_send[s, BLK:] = pack_halves(dq_rope[s * BLK : s * BLK + BLK])
    dq_recv[j] = dq_send[j]

    def dq_copy(i):
        return remote(dq_send.at[(j + i) % GRP], dq_recv.at[j], s_dq.at[i], r_dq.at[i], mate(i))

    for i in range(1, GRP):
        dq_copy(i).start()

    def add(ref, sem):
        arrived(ref, sem, beside)
        total[...] += ref[...].astype(F32)

    def row_sum(dy):
        for i in (1, 3, 2):
            d = SIDE * dy + (x + i) % SIDE - x

            @pl.when((d >= 1) & (d <= window))
            def _():
                add(far_recv.at[d], r_tf.at[d])

    for d in range(SLOT_LAG - 1, 3, -1):
        send_terms(d)

    @pl.when(y >= 2)
    def _():
        total[...] = far_send[2 * SIDE].astype(F32)
        row_sum(2)
        up_send[1] = total[...].astype(BF16)
        up_copy(1).start()

    for d in range(min(SLOT_LAG - 1, 3), 0, -1):
        send_terms(d)

    @pl.when(y >= 1)
    def _():
        total[...] = far_send[SIDE].astype(F32)
        row_sum(1)

        @pl.when(y + 1 < SIDE)
        def _():
            add(up_recv.at[1], r_up.at[1])

        up_send[0] = total[...].astype(BF16)
        up_copy(0).start()

    grad_w = dw_acc[...].T.astype(BF16)
    for i in range(groups):
        dw_send[i] = grad_w[i * w_rows : (i + 1) * w_rows]

    def dw_copy(i):
        return remote(dw_send.at[(g + i) % groups], dw_recv.at[i], s_dw.at[i], r_dw.at[i], other(i))

    def send_dw(i, carry):
        dw_copy(i).start()
        return carry

    lax.fori_loop(1, groups, send_dw, 0)

    total[...] = slot_sum(0)
    row_sum(0)

    @pl.when(corner_out)
    def _():
        add(far_recv.at[window], r_tf.at[window])

    @pl.when(y + 1 < SIDE)
    def _():
        add(up_recv.at[0], r_up.at[0])

    for t in range(zs):
        for c in range(COLS):
            z_send[t, c * z_rows : (c + 1) * z_rows] = total[
                c * BLK + t * z_rows : c * BLK + (t + 1) * z_rows
            ].astype(BF16)
        z_send[t, COLS * z_rows :] = total[LAT + t * zp_rows : LAT + (t + 1) * zp_rows].astype(BF16)

    def z_copy(i):
        return remote(z_send.at[(hz + i) % zs], z_recv.at[i], s_z.at[i], r_z.at[i], deep(i))

    for i in range(1, zs):
        z_copy(i).start()

    for i in range(1, GRP):
        arrived(dq_recv.at[(j + GRP - i) % GRP], r_dq.at[i], mate(i))
    columns = []
    for h in range(GRP):
        columns += [dq_recv[h, :BLK], unpack_halves(dq_recv[h, BLK:])]
    dq_out[...] = jnp.concatenate(columns, axis=1)

    z_sum = z_send[hz].astype(F32)
    for i in range(1, zs):
        arrived(z_recv.at[i], r_z.at[i], deep(i))
        z_sum = z_sum + z_recv[i].astype(F32)
    z_fin[hz] = z_sum.astype(BF16)

    def zf_copy(i):
        return remote(z_fin.at[hz], z_fin.at[hz], s_zf.at[i], r_zf.at[i], deep(i))

    for i in range(1, zs):
        zf_copy(i).start()

    dw_sum[...] = dw_send[g].astype(F32)

    def take_dw(i, carry):
        arrived(dw_recv.at[i], r_dw.at[i], other(i))
        dw_sum[...] += dw_recv[i].astype(F32)
        return carry

    lax.fori_loop(1, groups, take_dw, 0)

    def dwf_copy(i):
        rows = pl.ds(pl.multiple_of((j + i) % GRP * o_rows, o_rows), o_rows)
        return remote(dw_sum.at[rows], dw_fin.at[j], s_dwf.at[i], r_dwf.at[i], mate(i))

    for i in range(1, GRP):
        dwf_copy(i).start()
    dw_fin[j] = dw_sum[pl.ds(pl.multiple_of(j * o_rows, o_rows), o_rows)]

    for i in range(1, zs):
        arrived(z_fin.at[(hz + zs - i) % zs], r_zf.at[i], deep(i))
    packed = []
    for t in range(zs):
        for c in range(COLS):
            part = z_fin[t, c * z_rows : (c + 1) * z_rows].astype(F32)
            dlat_out[t * z_rows : (t + 1) * z_rows, c * BLK : (c + 1) * BLK] = part
        packed.append(z_fin[t, COLS * z_rows :].astype(F32))
    packed = jnp.concatenate(packed, axis=0).T
    drope_out[...] = jnp.concatenate([packed[:ROPE], packed[ROPE:]], axis=1)

    for i in range(1, GRP):
        arrived(dw_fin.at[(j + GRP - i) % GRP], r_dwf.at[i], mate(i))
    dw_out[...] = jnp.concatenate([dw_fin[h] for h in range(GRP)], axis=1)

    for i in range(1, GRP):
        q_copy(i).wait_send()
        dq_copy(i).wait_send()
        dwf_copy(i).wait_send()
    for i in range(1, zs):
        z_copy(i).wait_send()
        zf_copy(i).wait_send()

    def end_blocks(d, carry):
        @pl.when(g >= d)
        def _():
            own_copy(d).wait_send()
            near_copy(d).wait_send()
            pass_copy(d).wait_send()
            tc_copy(d).wait_send()
            tx_copy(d).wait_send()
            tn_copy(d).wait_send()

        @pl.when((d % SIDE != 0) & (g >= d))
        def _():
            tf_copy(d).wait_send()

        return carry

    lax.fori_loop(0, window + 1, end_blocks, 0)
    for dy in range(2):

        @pl.when((y + 1 < SIDE) & (y >= dy))
        def _():
            down_copy(dy).wait_send()

        @pl.when(y > dy)
        def _():
            up_copy(dy).wait_send()

    for dy in range(3):
        for i in (1, 3, 2):

            @pl.when(in_fan(dy, i))
            def _():
                fan_copy(dy, i).wait_send()

    @pl.when(corner_out)
    def _():
        corner_copy().wait_send()


    def end_dw(i, carry):
        dw_copy(i).wait_send()
        return carry

    lax.fori_loop(1, groups, end_dw, 0)


def solution(mesh):
    groups = mesh.shape["ctx"] // GRP
    zs = mesh.shape["head"]
    span = min(groups - 1, (MOST + GRP - 2) // GRP) + 1
    w_rows = LAT // groups
    z_piece = PIECE // zs
    vmem = pltpu.VMEM
    dma = pltpu.SemaphoreType.DMA
    scratch = [
        vmem((GRP, ROWS, 128), BF16),
        vmem((GRP, ROWS, 128), BF16),
        vmem((span, GRP, PIECE, 128), BF16),
        vmem((span, 2, KEYS // 2, 256), BF16),
        vmem((LAT, 256), BF16),
        vmem((KEYS, 256), BF16),
        vmem((KEYS, 256), BF16),
        vmem((KEYS, VDIM), BF16),
        vmem((span, 2, GRP, HALF, KEYS), F32),
        vmem((span, 2, GRP, HALF, KEYS), F32),
        vmem((span, 1, KEYS), F32),
        vmem((span, 1, KEYS), F32),
        vmem((span, 1, KEYS), F32),
        vmem((span, 1, KEYS), F32),
        vmem((1, KEYS), F32),
        vmem((NOPE, KEYS), F32),
        vmem((ROPE, KEYS), F32),
        vmem((256, LAT), F32),
        vmem((span, GRP, PIECE, 128), BF16),
        vmem((span, 2, PIECE, 128), BF16),
        vmem((span, PIECE, 128), BF16),
        vmem((span, PIECE, 128), BF16),
        vmem((span, PIECE, 128), BF16),
        vmem((span, PIECE, 128), BF16),
        vmem((2, PIECE, 128), BF16),
        vmem((2, PIECE, 128), BF16),
        vmem((PIECE, 128), F32),
        vmem((groups, w_rows, 256), BF16),
        vmem((groups, w_rows, 256), BF16),
        vmem((w_rows, 256), F32),
        vmem((GRP, w_rows // GRP, 256), F32),
        vmem((GRP, BLK + HALF, 128), BF16),
        vmem((GRP, BLK + HALF, 128), BF16),
        vmem((zs, z_piece, 128), BF16),
        vmem((zs, z_piece, 128), BF16),
        vmem((zs, z_piece, 128), BF16),
    ]
    scratch += [dma((1,)), dma((GRP,)), dma((GRP,)), dma((2,)), dma((3, SIDE)), dma((1,)), dma((span,))]
    for count in (*[span] * 7, 2, groups, GRP, GRP, zs, zs):
        scratch += [dma((count,)), dma((count,))]

    def local(query, latent, k_rope, d_out, w_kv, block_doc, block_order):
        whole = pl.BlockSpec(memory_space=pltpu.VMEM)
        scalars = pl.BlockSpec(memory_space=pltpu.SMEM)
        anywhere = pl.BlockSpec(memory_space=pl.ANY)
        results = pl.pallas_call(
            functools.partial(kernel, groups, zs),
            out_shape=(
                jax.ShapeDtypeStruct(query.shape, BF16),
                jax.ShapeDtypeStruct((BLK, LAT), F32),
                jax.ShapeDtypeStruct((ROPE, BLK), F32),
                jax.ShapeDtypeStruct((w_rows // GRP, GRP * 256), F32),
            ),
            in_specs=[whole] * 4 + [anywhere] + [scalars] * 2,
            out_specs=(whole,) * 4,
            scratch_shapes=scratch,
            compiler_params=pltpu.CompilerParams(
                collective_id=0, has_side_effects=True, vmem_limit_bytes=56 * 1024 * 1024
            ),
        )(query, latent, k_rope.T, d_out, w_kv, block_doc, block_order)
        d_query, d_latent, d_rope, d_w_kv = pl.pallas_call(
            keep,
            out_shape=tuple(jax.ShapeDtypeStruct(r.shape, r.dtype) for r in results),
            in_specs=[whole] * 4,
            out_specs=(whole,) * 4,
        )(*results)
        return d_query, d_latent, d_rope.T, d_w_kv

    return jax.shard_map(
        local,
        mesh=mesh,
        in_specs=(
            P("ctx", "head"),
            P("ctx", None),
            P("ctx", None),
            P("ctx", "head"),
            P(None, "head"),
            P(),
            P(),
        ),
        out_specs=(P("ctx", "head"), P("ctx", None), P("ctx", None), P("ctx", "head")),
        check_vma=False,
    )
```

```python
import functools
import math

import jax
import jax.numpy as jnp
from jax import lax
from jax.experimental import pallas as pl
from jax.experimental.pallas import tpu as pltpu
from jax.sharding import PartitionSpec as P

LAT = 512
ROPE = 64
NOPE = 128
VDIM = 128
BLK = 128
HEAD = NOPE + ROPE
HALF = BLK // 2
SIDE = 4
GRP = 4
KEYS = GRP * BLK
ROWS = 2 * BLK + HALF
COLS = LAT // BLK
PIECE = LAT + HALF
PASS_LAG, TILE_LAG = 3, 5
CHIP_LAG, SLOT_LAG = 2, 5
MOST = 36
SCALE = HEAD**-0.5
LOG2E = math.log2(math.e)
NEG = -1e30
MESH = pl.DeviceIdType.MESH
F32 = jnp.float32
BF16 = jnp.bfloat16


def nt(a, b):
    return lax.dot_general(a, b, (((1,), (1,)), ((), ())), preferred_element_type=F32)


def tn(a, b):
    return lax.dot_general(a, b, (((0,), (0,)), ((), ())), preferred_element_type=F32)


def nn(a, b):
    return jnp.dot(a, b, preferred_element_type=F32)


def pack_halves(rows):
    return jnp.concatenate([rows[:HALF], rows[HALF:]], axis=1)


def unpack_halves(rows):
    return jnp.concatenate([rows[:, :ROPE], rows[:, ROPE:]], axis=0)


def keep(a, b, c, d, a_out, b_out, c_out, d_out):
    for src, dst in ((a, a_out), (b, b_out), (c, c_out), (d, d_out)):
        dst[...] = src[...]


def kernel(
    groups,
    zs,
    query,
    latent,
    k_rope,
    d_out,
    w_kv,
    doc,
    order,
    dq_out,
    dlat_out,
    drope_out,
    dw_out,
    q_stage,
    q_buf,
    lat_buf,
    k_buf,
    w_head,
    q_lo,
    q_hi,
    g_out,
    p_buf,
    dp_buf,
    m_ref,
    mass_ref,
    ws_ref,
    fac_ref,
    delta_ref,
    dqn,
    dqr,
    dw_acc,
    terms,
    core_recv,
    near_send,
    near_recv,
    far_send,
    far_recv,
    up_send,
    up_recv,
    total,
    dw_send,
    dw_recv,
    dw_sum,
    dw_fin,
    dq_send,
    dq_recv,
    z_send,
    z_recv,
    z_fin,
    s_w,
    s_q,
    r_q,
    s_down,
    s_fan,
    s_corner,
    r_far,
    s_own,
    r_own,
    s_near,
    r_near,
    s_pass,
    r_pass,
    s_tc,
    r_tc,
    s_tx,
    r_tx,
    s_tn,
    r_tn,
    s_tf,
    r_tf,
    s_up,
    r_up,
    s_dw,
    r_dw,
    s_dwf,
    r_dwf,
    s_dq,
    r_dq,
    s_z,
    r_z,
    s_zf,
    r_zf,
):
    ctx = lax.axis_index("ctx")
    hz = lax.axis_index("head")
    g = ctx // GRP
    j = ctx % GRP
    z_lo = j // 2
    core = j % 2
    j_core = 2 * z_lo + 1 - core
    j_near = 2 * (1 - z_lo) + core
    j_next = 2 * (1 - z_lo) + 1 - core
    window = min(groups - 1, (MOST + GRP - 2) // GRP)
    y = g // SIDE
    x = g % SIDE
    w_rows = LAT // groups
    o_rows = w_rows // GRP
    z_rows = BLK // zs
    zp_rows = HALF // zs

    def mate(i):
        return ((g * GRP + (j + i) % GRP), hz)

    def other(i):
        return (((g + i) % groups) * GRP + j, hz)

    def deep(i):
        return (ctx, (hz + i) % zs)

    beside = (g * GRP + j_core, hz)
    ahead = (g * GRP + j_near, (hz + z_lo + core * (zs - 1)) % zs)
    behind = (g * GRP + j_near, (hz + z_lo + (1 - core) * (zs - 1)) % zs)

    def remote(src, dst, send, recv, to):
        return pltpu.make_async_remote_copy(
            src_ref=src, dst_ref=dst, send_sem=send, recv_sem=recv, device_id=to, device_id_type=MESH
        )

    def arrived(ref, sem, to):
        remote(ref, ref, sem, sem, to).wait_recv()

    columns = pl.ds(pl.multiple_of(j * 256, 256), 256)
    weights = pltpu.make_async_copy(w_kv.at[:, columns], w_head, s_w.at[0])
    weights.start()
    barrier = pltpu.get_barrier_semaphore()
    for i in range(1, GRP):
        pl.semaphore_signal(barrier, inc=1, device_id=mate(i), device_id_type=MESH)
    for i in range(1, zs):
        pl.semaphore_signal(barrier, inc=1, device_id=deep(i), device_id_type=MESH)
    pl.semaphore_signal(barrier, inc=1, device_id=ahead, device_id_type=MESH)
    pl.semaphore_signal(barrier, inc=1, device_id=behind, device_id_type=MESH)

    def greet(i, carry):
        pl.semaphore_signal(barrier, inc=1, device_id=other(i), device_id_type=MESH)
        return carry

    lax.fori_loop(1, groups, greet, 0)

    for c in range(COLS):
        lat_buf[0, j, c * BLK : (c + 1) * BLK] = latent[:, c * BLK : (c + 1) * BLK]
    lat_buf[0, j, LAT:] = pack_halves(k_rope[...].astype(F32).T.astype(BF16))
    for h in range(GRP):
        q_stage[h, :BLK] = query[:, HEAD * h : HEAD * h + NOPE]
        q_stage[h, BLK : 2 * BLK] = d_out[:, VDIM * h : VDIM * h + VDIM]
        q_stage[h, 2 * BLK :] = pack_halves(query[:, HEAD * h + NOPE : HEAD * h + HEAD])

    pl.semaphore_wait(barrier, GRP - 1 + zs - 1 + 2 + groups - 1)

    def row_mate(i):
        return ((g - x + (x + i) % SIDE) * GRP + j, hz)

    def down_copy(dy):
        here, there = SIDE * dy, SIDE * (dy + 1)
        to = ((g + SIDE) * GRP + j, hz)
        return remote(lat_buf.at[here, j], lat_buf.at[there, j], s_down.at[dy], r_far.at[there], to)

    def fan_copy(dy, i):
        d = SIDE * dy + (x + i) % SIDE - x
        return remote(lat_buf.at[SIDE * dy, j], lat_buf.at[d, j], s_fan.at[dy, i], r_far.at[d], row_mate(i))

    def in_fan(dy, i):
        d = SIDE * dy + (x + i) % SIDE - x
        return (y >= dy) & (d >= 1) & (d <= window)

    corner_out = (y == 0) & (x == SIDE - 1)

    def corner_copy():
        return remote(lat_buf.at[0, j], lat_buf.at[window, j], s_corner.at[0], r_far.at[window], other(window))

    def fan(dy):
        for i in (1, 3, 2):

            @pl.when(in_fan(dy, i))
            def _():
                fan_copy(dy, i).start()

    def own_copy(d):
        return remote(lat_buf.at[d, j], lat_buf.at[d, j], s_own.at[d], r_own.at[d], beside)

    def near_copy(d):
        return remote(lat_buf.at[d, j], lat_buf.at[d, j], s_near.at[d], r_near.at[d], ahead)

    def pass_copy(d):
        return remote(lat_buf.at[d, j_near], lat_buf.at[d, j_near], s_pass.at[d], r_pass.at[d], beside)

    def q_copy(i):
        return remote(q_stage.at[(j + i) % GRP], q_buf.at[j], s_q.at[i], r_q.at[i], mate(i))

    near_copy(0).start()
    own_copy(0).start()

    @pl.when(y + 1 < SIDE)
    def _():
        down_copy(0).start()

    fan(0)

    @pl.when(corner_out)
    def _():
        corner_copy().start()

    for i in range(1, GRP):
        q_copy(i).start()
    q_buf[j] = q_stage[j]

    slot_of = lax.broadcasted_iota(jnp.int32, (1, KEYS), 1) // BLK
    in_slot = lax.broadcasted_iota(jnp.int32, (1, KEYS), 1) % BLK
    q_pos = jnp.zeros((1, KEYS), jnp.int32)
    q_doc = jnp.zeros((1, KEYS), jnp.int32)
    for s in range(GRP):
        block = order[GRP * g + s]
        q_pos = jnp.where(slot_of == s, block * BLK + in_slot, q_pos)
        q_doc = jnp.where(slot_of == s, doc[block], q_doc)

    m_ref[...] = jnp.full(m_ref.shape, NEG, F32)
    mass_ref[...] = jnp.zeros(mass_ref.shape, F32)
    ws_ref[...] = jnp.zeros(ws_ref.shape, F32)

    def latents_of(d):
        return jnp.concatenate(
            [
                jnp.concatenate([lat_buf[d, s, c * BLK : (c + 1) * BLK] for c in range(COLS)], axis=1)
                for s in range(GRP)
            ],
            axis=0,
        )

    def half_rows(rows, half):
        return jnp.concatenate(
            [rows[s * BLK + half * HALF : s * BLK + half * HALF + HALF] for s in range(GRP)], axis=0
        )

    def scores_tile(d, local):
        kv = nn(latents_of(d), w_head[...]).astype(BF16)
        rope = jnp.concatenate([lat_buf[d, s, LAT:] for s in range(GRP)], axis=0)
        top = jnp.full((8, KEYS), NEG, F32)
        for half in range(2):
            k_buf[d, half] = jnp.concatenate([half_rows(kv[:, :NOPE], half), rope], axis=1)
            scores = nt(k_buf[d, half], (q_lo, q_hi)[half][...])
            for s in range(GRP):
                block = order[GRP * (g - d) + s]
                same = q_doc == doc[block]
                part = scores[s * HALF : s * HALF + HALF] * (SCALE * LOG2E)
                if local:
                    pos = lax.broadcasted_iota(jnp.int32, (HALF, 1), 0) + (block * BLK + half * HALF)
                    part = jnp.where(same & (pos <= q_pos), part, NEG)
                else:
                    part = part + jnp.where(same, 0.0, NEG)
                p_buf[d, half, s] = part
                top = jnp.maximum(top, jnp.max(part.reshape(HALF // 8, 8, KEYS), axis=0))
        peak = jnp.max(top, axis=0, keepdims=True)
        mass = jnp.zeros((8, KEYS), F32)
        weighted = jnp.zeros((8, KEYS), F32)
        for half in range(2):
            dp = nt(half_rows(kv[:, NOPE:], half), g_out[...])
            for s in range(GRP):
                here = dp[s * HALF : s * HALF + HALF]
                p = jnp.exp2(p_buf[d, half, s] - peak)
                p_buf[d, half, s] = p
                dp_buf[d, half, s] = here
                mass = mass + jnp.sum(p.reshape(HALF // 8, 8, KEYS), axis=0)
                weighted = weighted + jnp.sum((p * here).reshape(HALF // 8, 8, KEYS), axis=0)
        m_ref[d] = peak
        mass_ref[d] = jnp.sum(mass, axis=0, keepdims=True)
        ws_ref[d] = jnp.sum(weighted, axis=0, keepdims=True)

    def spread(d):
        @pl.when((d <= window) & (g >= d) & (d % SIDE != 0))
        def _():
            arrived(lat_buf.at[d, j], r_far.at[d], beside)
            near_copy(d).start()
            own_copy(d).start()

    def hand_on(d):
        @pl.when((d >= 0) & (d <= window) & (g >= d))
        def _():
            arrived(lat_buf.at[d, j_near], r_near.at[d], beside)
            pass_copy(d).start()

    def whole(d):
        arrived(lat_buf.at[d, j_core], r_own.at[d], beside)
        arrived(lat_buf.at[d, j_next], r_pass.at[d], beside)

    hand_on(0)

    @pl.when(y >= 1)
    def _():
        arrived(lat_buf.at[SIDE, j], r_far.at[SIDE], beside)

        @pl.when(y + 1 < SIDE)
        def _():
            down_copy(1).start()

        near_copy(SIDE).start()
        own_copy(SIDE).start()

    fan(1)
    for i in range(1, GRP):
        arrived(q_buf.at[(j + GRP - i) % GRP], r_q.at[i], mate(i))
    blank = jnp.zeros((HALF, ROPE), BF16)
    for s in range(GRP):
        at = s * BLK
        pair = q_buf[s, 2 * BLK :]
        first, second = pair[:, :ROPE], pair[:, ROPE:]
        q_lo[at : at + BLK, :NOPE] = q_buf[s, :BLK]
        q_hi[at : at + BLK, :NOPE] = q_buf[s, :BLK]
        g_out[at : at + BLK] = q_buf[s, BLK : 2 * BLK]
        q_lo[at : at + HALF, NOPE:] = jnp.concatenate([first, blank], axis=1)
        q_lo[at + HALF : at + BLK, NOPE:] = jnp.concatenate([second, blank], axis=1)
        q_hi[at : at + HALF, NOPE:] = jnp.concatenate([blank, first], axis=1)
        q_hi[at + HALF : at + BLK, NOPE:] = jnp.concatenate([blank, second], axis=1)
    whole(0)
    weights.wait()
    scores_tile(0, True)

    @pl.when(y >= 2)
    def _():
        arrived(lat_buf.at[2 * SIDE, j], r_far.at[2 * SIDE], beside)
        near_copy(2 * SIDE).start()
        own_copy(2 * SIDE).start()

    fan(2)

    def far_scores(i, carry):
        spread(i)

        @pl.when(i > PASS_LAG)
        def _():
            hand_on(i - PASS_LAG)

        @pl.when((i > TILE_LAG) & (g >= i - TILE_LAG))
        def _():
            whole(i - TILE_LAG)
            scores_tile(i - TILE_LAG, False)

        return carry

    lax.fori_loop(1, window + TILE_LAG + 1, far_scores, 0)

    peak = jnp.max(m_ref[...], axis=0)
    factors = jnp.exp2(m_ref[...] - peak[None])
    mass = jnp.sum(mass_ref[...] * factors, axis=0)
    weighted = jnp.sum(ws_ref[...] * factors, axis=0)
    fac_ref[...] = factors / mass[None]
    delta_ref[...] = weighted / mass
    dqn[...] = jnp.zeros(dqn.shape, F32)
    dqr[...] = jnp.zeros(dqr.shape, F32)
    dw_acc[...] = jnp.zeros(dw_acc.shape, F32)

    def grads_tile(d):
        factor = fac_ref[d]
        delta = delta_ref[...]
        rope_sum = None
        pairs = []
        for half in range(2):
            mixed, probs = [], []
            for s in range(GRP):
                p = p_buf[d, half, s] * factor
                mixed.append((p * (dp_buf[d, half, s] - delta)).astype(BF16))
                probs.append(p.astype(BF16))
            mixed = jnp.concatenate(mixed, axis=0)
            probs = jnp.concatenate(probs, axis=0)
            d_keys = nn(mixed, (q_lo, q_hi)[half][...]) * SCALE
            d_values = nn(probs, g_out[...])
            rope_sum = d_keys[:, NOPE:] if half == 0 else rope_sum + d_keys[:, NOPE:]
            pairs.append(jnp.concatenate([d_keys[:, :NOPE], d_values], axis=1).astype(BF16))
            dq = tn(k_buf[d, half], mixed)
            dqn[...] += dq[:NOPE]
            dqr[...] += dq[NOPE + half * ROPE : NOPE + half * ROPE + ROPE]
        pairs = jnp.concatenate(
            [pairs[half][s * HALF : s * HALF + HALF] for s in range(GRP) for half in range(2)], axis=0
        )
        d_lat = nt(pairs, w_head[...])
        for s in range(GRP):
            for c in range(COLS):
                part = d_lat[s * BLK : (s + 1) * BLK, c * BLK : (c + 1) * BLK]
                terms[d, s, c * BLK : (c + 1) * BLK] = part.astype(BF16)
            terms[d, s, LAT:] = rope_sum[s * HALF : s * HALF + HALF].astype(BF16)
        dw_acc[...] += tn(pairs, latents_of(d))

    def tc_copy(d):
        return remote(terms.at[d, j_core], core_recv.at[d, 0], s_tc.at[d], r_tc.at[d], beside)

    def tx_copy(d):
        return remote(terms.at[d, j_next], core_recv.at[d, 1], s_tx.at[d], r_tx.at[d], beside)

    def tn_copy(d):
        return remote(near_send.at[d], near_recv.at[d], s_tn.at[d], r_tn.at[d], behind)

    def tf_copy(d):
        return remote(far_send.at[d], far_recv.at[d], s_tf.at[d], r_tf.at[d], row_mate(4 * SIDE - d))

    def tf_corner():
        d = window
        return remote(far_send.at[d], far_recv.at[d], s_tf.at[d], r_tf.at[d], other(groups - d))

    def up_copy(dy):
        to = ((g - SIDE) * GRP + j, hz)
        return remote(up_send.at[dy], up_recv.at[dy], s_up.at[dy], r_up.at[dy], to)

    def chip_sum(d):
        @pl.when((d <= window) & (g >= d))
        def _():
            arrived(core_recv.at[d, 1], r_tx.at[d], beside)
            near_send[d] = (terms[d, j_near].astype(F32) + core_recv[d, 1].astype(F32)).astype(BF16)
            tn_copy(d).start()

    def slot_sum(d):
        arrived(core_recv.at[d, 0], r_tc.at[d], beside)
        arrived(near_recv.at[d], r_tn.at[d], beside)
        return terms[d, j].astype(F32) + core_recv[d, 0].astype(F32) + near_recv[d].astype(F32)

    def send_terms(d):
        @pl.when((d <= window) & (g >= d))
        def _():
            far_send[d] = slot_sum(d).astype(BF16)

            @pl.when((d % SIDE != 0) & ((d < window) | (x > 0)))
            def _():
                tf_copy(d).start()

            @pl.when((d == window) & (x == 0))
            def _():
                tf_corner().start()

    def far_grads(step, carry):
        d = window - step

        @pl.when(g >= d)
        def _():
            grads_tile(d)
            tx_copy(d).start()
            tc_copy(d).start()

        chip_sum(d + CHIP_LAG)
        send_terms(d + SLOT_LAG)
        return carry

    lax.fori_loop(0, window + 1, far_grads, 0)
    for d in range(CHIP_LAG - 1, -1, -1):
        chip_sum(d)

    dq_nope = (dqn[...] * SCALE).T.astype(BF16)
    dq_rope = (dqr[...] * SCALE).T.astype(BF16)
    for s in range(GRP):
        dq_send[s, :BLK] = dq_nope[s * BLK : s * BLK + BLK]
        dq_send[s, BLK:] = pack_halves(dq_rope[s * BLK : s * BLK + BLK])
    dq_recv[j] = dq_send[j]

    def dq_copy(i):
        return remote(dq_send.at[(j + i) % GRP], dq_recv.at[j], s_dq.at[i], r_dq.at[i], mate(i))

    for i in range(1, GRP):
        dq_copy(i).start()

    def add(ref, sem):
        arrived(ref, sem, beside)
        total[...] += ref[...].astype(F32)

    def row_sum(dy):
        for i in (1, 3, 2):
            d = SIDE * dy + (x + i) % SIDE - x

            @pl.when((d >= 1) & (d <= window))
            def _():
                add(far_recv.at[d], r_tf.at[d])

    for d in range(SLOT_LAG - 1, 3, -1):
        send_terms(d)

    @pl.when(y >= 2)
    def _():
        total[...] = far_send[2 * SIDE].astype(F32)
        row_sum(2)
        up_send[1] = total[...].astype(BF16)
        up_copy(1).start()

    for d in range(min(SLOT_LAG - 1, 3), 0, -1):
        send_terms(d)

    @pl.when(y >= 1)
    def _():
        total[...] = far_send[SIDE].astype(F32)
        row_sum(1)

        @pl.when(y + 1 < SIDE)
        def _():
            add(up_recv.at[1], r_up.at[1])

        up_send[0] = total[...].astype(BF16)
        up_copy(0).start()

    grad_w = dw_acc[...].T.astype(BF16)
    for i in range(groups):
        dw_send[i] = grad_w[i * w_rows : (i + 1) * w_rows]

    def dw_copy(i):
        return remote(dw_send.at[(g + i) % groups], dw_recv.at[i], s_dw.at[i], r_dw.at[i], other(i))

    def send_dw(i, carry):
        dw_copy(i).start()
        return carry

    lax.fori_loop(1, groups, send_dw, 0)

    total[...] = slot_sum(0)
    row_sum(0)

    @pl.when(corner_out)
    def _():
        add(far_recv.at[window], r_tf.at[window])

    @pl.when(y + 1 < SIDE)
    def _():
        add(up_recv.at[0], r_up.at[0])

    for t in range(zs):
        for c in range(COLS):
            z_send[t, c * z_rows : (c + 1) * z_rows] = total[
                c * BLK + t * z_rows : c * BLK + (t + 1) * z_rows
            ].astype(BF16)
        z_send[t, COLS * z_rows :] = total[LAT + t * zp_rows : LAT + (t + 1) * zp_rows].astype(BF16)

    def z_copy(i):
        return remote(z_send.at[(hz + i) % zs], z_recv.at[i], s_z.at[i], r_z.at[i], deep(i))

    for i in range(1, zs):
        z_copy(i).start()

    for i in range(1, GRP):
        q_copy(i).wait_send()
        dq_copy(i).wait_send()

    def end_blocks(d, carry):
        @pl.when(g >= d)
        def _():
            own_copy(d).wait_send()
            near_copy(d).wait_send()
            pass_copy(d).wait_send()
            tc_copy(d).wait_send()
            tx_copy(d).wait_send()
            tn_copy(d).wait_send()

        @pl.when((d % SIDE != 0) & (g >= d))
        def _():
            tf_copy(d).wait_send()

        return carry

    lax.fori_loop(0, window + 1, end_blocks, 0)
    for dy in range(2):

        @pl.when((y + 1 < SIDE) & (y >= dy))
        def _():
            down_copy(dy).wait_send()

        @pl.when(y > dy)
        def _():
            up_copy(dy).wait_send()

    for dy in range(3):
        for i in (1, 3, 2):

            @pl.when(in_fan(dy, i))
            def _():
                fan_copy(dy, i).wait_send()

    @pl.when(corner_out)
    def _():
        corner_copy().wait_send()


    for i in range(1, GRP):
        arrived(dq_recv.at[(j + GRP - i) % GRP], r_dq.at[i], mate(i))
    columns = []
    for h in range(GRP):
        columns += [dq_recv[h, :BLK], unpack_halves(dq_recv[h, BLK:])]
    dq_out[...] = jnp.concatenate(columns, axis=1)

    z_sum = z_send[hz].astype(F32)
    for i in range(1, zs):
        arrived(z_recv.at[i], r_z.at[i], deep(i))
        z_sum = z_sum + z_recv[i].astype(F32)
    z_fin[hz] = z_sum.astype(BF16)

    def zf_copy(i):
        return remote(z_fin.at[hz], z_fin.at[hz], s_zf.at[i], r_zf.at[i], deep(i))

    for i in range(1, zs):
        zf_copy(i).start()

    dw_sum[...] = dw_send[g].astype(F32)

    def take_dw(i, carry):
        arrived(dw_recv.at[i], r_dw.at[i], other(i))
        dw_sum[...] += dw_recv[i].astype(F32)
        return carry

    lax.fori_loop(1, groups, take_dw, 0)

    def dwf_copy(i):
        rows = pl.ds(pl.multiple_of((j + i) % GRP * o_rows, o_rows), o_rows)
        return remote(dw_sum.at[rows], dw_fin.at[j], s_dwf.at[i], r_dwf.at[i], mate(i))

    for i in range(1, GRP):
        dwf_copy(i).start()
    dw_fin[j] = dw_sum[pl.ds(pl.multiple_of(j * o_rows, o_rows), o_rows)]

    for i in range(1, zs):
        arrived(z_fin.at[(hz + zs - i) % zs], r_zf.at[i], deep(i))
    packed = []
    for t in range(zs):
        for c in range(COLS):
            part = z_fin[t, c * z_rows : (c + 1) * z_rows].astype(F32)
            dlat_out[t * z_rows : (t + 1) * z_rows, c * BLK : (c + 1) * BLK] = part
        packed.append(z_fin[t, COLS * z_rows :].astype(F32))
    packed = jnp.concatenate(packed, axis=0).T
    drope_out[...] = jnp.concatenate([packed[:ROPE], packed[ROPE:]], axis=1)

    for i in range(1, GRP):
        arrived(dw_fin.at[(j + GRP - i) % GRP], r_dwf.at[i], mate(i))
    dw_out[...] = jnp.concatenate([dw_fin[h] for h in range(GRP)], axis=1)

    for i in range(1, GRP):
        dwf_copy(i).wait_send()
    for i in range(1, zs):
        z_copy(i).wait_send()
        zf_copy(i).wait_send()

    def end_dw(i, carry):
        dw_copy(i).wait_send()
        return carry

    lax.fori_loop(1, groups, end_dw, 0)


def solution(mesh):
    groups = mesh.shape["ctx"] // GRP
    zs = mesh.shape["head"]
    span = min(groups - 1, (MOST + GRP - 2) // GRP) + 1
    w_rows = LAT // groups
    z_piece = PIECE // zs
    vmem = pltpu.VMEM
    dma = pltpu.SemaphoreType.DMA
    scratch = [
        vmem((GRP, ROWS, 128), BF16),
        vmem((GRP, ROWS, 128), BF16),
        vmem((span, GRP, PIECE, 128), BF16),
        vmem((span, 2, KEYS // 2, 256), BF16),
        vmem((LAT, 256), BF16),
        vmem((KEYS, 256), BF16),
        vmem((KEYS, 256), BF16),
        vmem((KEYS, VDIM), BF16),
        vmem((span, 2, GRP, HALF, KEYS), F32),
        vmem((span, 2, GRP, HALF, KEYS), F32),
        vmem((span, 1, KEYS), F32),
        vmem((span, 1, KEYS), F32),
        vmem((span, 1, KEYS), F32),
        vmem((span, 1, KEYS), F32),
        vmem((1, KEYS), F32),
        vmem((NOPE, KEYS), F32),
        vmem((ROPE, KEYS), F32),
        vmem((256, LAT), F32),
        vmem((span, GRP, PIECE, 128), BF16),
        vmem((span, 2, PIECE, 128), BF16),
        vmem((span, PIECE, 128), BF16),
        vmem((span, PIECE, 128), BF16),
        vmem((span, PIECE, 128), BF16),
        vmem((span, PIECE, 128), BF16),
        vmem((2, PIECE, 128), BF16),
        vmem((2, PIECE, 128), BF16),
        vmem((PIECE, 128), F32),
        vmem((groups, w_rows, 256), BF16),
        vmem((groups, w_rows, 256), BF16),
        vmem((w_rows, 256), F32),
        vmem((GRP, w_rows // GRP, 256), F32),
        vmem((GRP, BLK + HALF, 128), BF16),
        vmem((GRP, BLK + HALF, 128), BF16),
        vmem((zs, z_piece, 128), BF16),
        vmem((zs, z_piece, 128), BF16),
        vmem((zs, z_piece, 128), BF16),
    ]
    scratch += [dma((1,)), dma((GRP,)), dma((GRP,)), dma((2,)), dma((3, SIDE)), dma((1,)), dma((span,))]
    for count in (*[span] * 7, 2, groups, GRP, GRP, zs, zs):
        scratch += [dma((count,)), dma((count,))]

    def local(query, latent, k_rope, d_out, w_kv, block_doc, block_order):
        whole = pl.BlockSpec(memory_space=pltpu.VMEM)
        scalars = pl.BlockSpec(memory_space=pltpu.SMEM)
        anywhere = pl.BlockSpec(memory_space=pl.ANY)
        results = pl.pallas_call(
            functools.partial(kernel, groups, zs),
            out_shape=(
                jax.ShapeDtypeStruct(query.shape, BF16),
                jax.ShapeDtypeStruct((BLK, LAT), F32),
                jax.ShapeDtypeStruct((ROPE, BLK), F32),
                jax.ShapeDtypeStruct((w_rows // GRP, GRP * 256), F32),
            ),
            in_specs=[whole] * 4 + [anywhere] + [scalars] * 2,
            out_specs=(whole,) * 4,
            scratch_shapes=scratch,
            compiler_params=pltpu.CompilerParams(
                collective_id=0, has_side_effects=True, vmem_limit_bytes=56 * 1024 * 1024
            ),
        )(query, latent, k_rope.T, d_out, w_kv, block_doc, block_order)
        d_query, d_latent, d_rope, d_w_kv = pl.pallas_call(
            keep,
            out_shape=tuple(jax.ShapeDtypeStruct(r.shape, r.dtype) for r in results),
            in_specs=[whole] * 4,
            out_specs=(whole,) * 4,
        )(*results)
        return d_query, d_latent, d_rope.T, d_w_kv

    return jax.shard_map(
        local,
        mesh=mesh,
        in_specs=(
            P("ctx", "head"),
            P("ctx", None),
            P("ctx", None),
            P("ctx", "head"),
            P(None, "head"),
            P(),
            P(),
        ),
        out_specs=(P("ctx", "head"), P("ctx", None), P("ctx", None), P("ctx", "head")),
        check_vma=False,
    )
```
